256 devices in a mesh: grp: 8 (over x, core), mem: 32 (over y, z).
Axes of the slice: x: 4, y: 4, z: 8, core: 2. Of those that a mesh axis runs over, the one named last changes fastest.
Arguments:
- amp_plus: bfloat16 [24576, 4096], P('mem', 'grp'), may hold values from -6 to 6
- amp_minus: bfloat16 [24576, 4096], P('mem', 'grp'), may hold values from -6 to 6
- ints_plus: bfloat16 [8192, 4096], P('grp', 'mem'), may hold values from -0.125 to 0.125
- ints_minus: bfloat16 [8192, 4096], P('grp', 'mem'), may hold values from -0.125 to 0.125
- sym_ij: int32 [192], P('mem'), may hold values from 0 to 1
- sym_ab: int32 [64], P('grp'), may hold values from 0 to 1
- sym_cd: int32 [32], replicated, may hold values from 0 to 1
- amp_mask: int32 [192, 32], P('mem'), may hold values 0 or 1
Outputs:
- ladder: bfloat16 [24576, 8192], P('mem', 'grp')
The draws below stay inside these ranges and needn't reach their ends.
All inputs are finite; a program needn't handle non-finite values. No bound on the sum of `amp_mask` on one device may be relied on, other than what follows from the above.
Results may differ from the reference program's by a relative error of at most 0.001.
Values may be sent and summed in bfloat16 or wider, within the bound.
No kernel may reach another device: no remote copies, remote signals or barrier semaphores. Data moves between devices by JAX's collectives and lax.ppermute only.
A program may use at most 128 MiB of HBM per device.

```python
import jax
import jax.numpy as jnp
from jax import lax

BLK = 128
AB_GRP = 1024
IJ = 24576
AB = 8192
CD = 4096


def set_ends(values, rng, low, top_value):
    longest = values.shape.index(max(values.shape))
    spots = []
    for shift in (0, 1):
        where = [jax.random.randint(jax.random.fold_in(rng, axis), (), 0, length) for axis, length in enumerate(values.shape)]
        where[longest] = (where[longest] + shift) % values.shape[longest]
        spots.append(tuple(where))
    return values.at[spots[0]].set(low).at[spots[1]].set(top_value)


def block_scale(own_key, extent, split, low, top_value):
    level = 1.0
    for axis_at, parts in split:
        draws = jax.random.uniform(jax.random.fold_in(jax.random.fold_in(own_key, 6), axis_at), (parts,), jnp.float32, low / len(split), top_value / len(split))
        level = level * jnp.repeat(jnp.exp(draws), extent[axis_at] // parts).reshape((-1,) + (1,) * (len(extent) - 1 - axis_at))
    return level


def normal_values(rng, shape, width, bound, split=(), kind=jnp.bfloat16):
    drawn = width * jax.random.normal(rng, shape, jnp.float32)
    if split:
        drawn = drawn * block_scale(rng, shape, split, -0.22, 0.18)
    return jnp.clip(drawn, -bound, bound).astype(kind)


def setup_inputs(seed: int = 0) -> dict:
    key_of = jax.random.split(jax.random.key(seed), 9)
    amp_plus = normal_values(key_of[0], (IJ, CD), 1.0, 6.0, ((0, 32), (1, 8)))
    amp_minus = normal_values(key_of[1], (IJ, CD), 1.0, 6.0, ((0, 32), (1, 8)))
    ints_plus = normal_values(key_of[2], (AB, CD), (CD // 2) ** -0.5, 0.125, ((0, 8), (1, 32)))
    ints_minus = normal_values(key_of[3], (AB, CD), (CD // 2) ** -0.5, 0.125, ((0, 8), (1, 32)))
    sym_ij = set_ends(jax.random.randint(key_of[4], (IJ // BLK,), 0, 2), jax.random.fold_in(key_of[4], 1), 0, 1).astype(jnp.int32)
    sym_ab = set_ends(jax.random.randint(key_of[5], (AB // BLK,), 0, 2), jax.random.fold_in(key_of[5], 1), 0, 1).astype(jnp.int32)
    sym_cd = set_ends(jax.random.randint(key_of[6], (CD // BLK,), 0, 2), jax.random.fold_in(key_of[6], 1), 0, 1).astype(jnp.int32)
    amp_mask = set_ends((jax.random.randint(key_of[7], (IJ // BLK, CD // BLK), 0, 4) < 3).astype(jnp.int32), jax.random.fold_in(key_of[7], 1), 0, 1)
    return dict(amp_plus=amp_plus, amp_minus=amp_minus, ints_plus=ints_plus, ints_minus=ints_minus, sym_ij=sym_ij, sym_ab=sym_ab, sym_cd=sym_cd, amp_mask=amp_mask)


def mask_amps(amps, sym_ij, sym_cd, amp_mask):
    flags = ((sym_ij[:, None] == sym_cd[None, :]) & (amp_mask == 1)).astype(amps.dtype)
    rows_t = amps.shape[0] // BLK
    cols_t = amps.shape[1] // BLK
    shaped = amps.reshape(rows_t, BLK, cols_t, BLK) * flags[:, None, :, None]
    return shaped.reshape(amps.shape)


def mask_ints(ints, sym_ab, sym_cd):
    flags = (sym_ab[:, None] == sym_cd[None, :]).astype(ints.dtype)
    rows_t = ints.shape[0] // BLK
    cols_t = ints.shape[1] // BLK
    shaped = ints.reshape(rows_t, BLK, cols_t, BLK) * flags[:, None, :, None]
    return shaped.reshape(ints.shape)


def reference(amp_plus, amp_minus, ints_plus, ints_minus, sym_ij, sym_ab, sym_cd, amp_mask):
    tplus = mask_amps(amp_plus, sym_ij, sym_cd, amp_mask)
    tminus = mask_amps(amp_minus, sym_ij, sym_cd, amp_mask)
    vplus = mask_ints(ints_plus, sym_ab, sym_cd)
    vminus = mask_ints(ints_minus, sym_ab, sym_cd)
    blocks = AB // AB_GRP
    vplus = vplus.reshape(blocks, AB_GRP, CD)
    vminus = vminus.reshape(blocks, AB_GRP, CD)
    dims = (((1,), (1,)), ((), ()))

    def one_block(panels):
        zplus = lax.dot_general(tplus, panels[0], dims, preferred_element_type=jnp.float32)
        zminus = lax.dot_general(tminus, panels[1], dims, preferred_element_type=jnp.float32)
        return (0.5 * (zplus + zminus)).astype(jnp.bfloat16)

    stacked = lax.map(one_block, (vplus, vminus))
    return jnp.transpose(stacked, (1, 0, 2)).reshape(IJ, AB)
```

```python
import jax
import jax.numpy as jnp
from jax import lax
from jax.experimental import pallas as pl
from jax.experimental.pallas import tpu as pltpu
from jax.sharding import PartitionSpec as P

BLK = 128
AXES = ("grp", "mem")
NX, NY, NZ = 4, 4, 8


def perm_of(dx, dy, dz, swap=0):
    pairs = []
    for x in range(NX):
        for core in range(2):
            sign = 1 if core == 0 else -1
            for y in range(NY):
                for z in range(NZ):
                    src = (2 * x + core) * 32 + 8 * y + z
                    x2, y2, z2 = (x + sign * dx) % NX, (y + sign * dy) % NY, (z + sign * dz) % NZ
                    core2 = core ^ swap
                    pairs.append((src, (2 * x2 + core2) * 32 + 8 * y2 + z2))
    return pairs


PERM_X, PERM_Y, PERM_Z = perm_of(1, 0, 0), perm_of(0, 1, 0), perm_of(0, 0, 1)
PERM_C = perm_of(0, 0, 0, 1)


def move(values, perm):
    return lax.ppermute(values, AXES, perm)


def place_kernel(pos_ref, flag_ref, mine_ref, other_ref, plus_in, minus_in, plus_out, minus_out, stage, sems):
    del plus_in, minus_in
    copies = []
    for src, block in enumerate((mine_ref, other_ref)):
        for panel, target in enumerate((plus_out, minus_out)):
            for col in range(4):
                tile = src * 4 + col
                for row in range(6):
                    rows = slice(row * BLK, (row + 1) * BLK)
                    kept = block[panel, rows, col * BLK:(col + 1) * BLK]
                    on = flag_ref[row, tile] == 1
                    stage[panel, tile, rows, :] = jnp.where(on, kept, jnp.zeros_like(kept))
                at = pl.multiple_of(pos_ref[panel, tile] * BLK, BLK)
                copy = pltpu.make_async_copy(
                    stage.at[panel, tile], target.at[:, pl.ds(at, BLK)], sems.at[panel, tile]
                )
                copy.start()
                copies.append(copy)
    for copy in copies:
        copy.wait()


def place(pos, flags, mine, other, plus, minus):
    any_spec = pl.BlockSpec(memory_space=pl.ANY)
    smem = pl.BlockSpec(memory_space=pltpu.SMEM)
    vmem = pl.BlockSpec(memory_space=pltpu.VMEM)
    return pl.pallas_call(
        place_kernel,
        out_shape=(jax.ShapeDtypeStruct(plus.shape, plus.dtype), jax.ShapeDtypeStruct(minus.shape, minus.dtype)),
        in_specs=[smem, smem, vmem, vmem, any_spec, any_spec],
        out_specs=(any_spec, any_spec),
        scratch_shapes=[pltpu.VMEM((2, 8, 768, BLK), jnp.bfloat16), pltpu.SemaphoreType.DMA((2, 8))],
        input_output_aliases={4: 0, 5: 1},
        compiler_params=pltpu.CompilerParams(vmem_limit_bytes=32 * 2**20),
        cost_estimate=pl.CostEstimate(flops=0, bytes_accessed=7 * 2**20, transcendentals=0),
    )(pos, flags, mine, other, plus, minus)


def empty_kernel(plus_out, minus_out):
    del plus_out, minus_out


def empty(shape):
    any_spec = pl.BlockSpec(memory_space=pl.ANY)
    one = jax.ShapeDtypeStruct(shape, jnp.bfloat16)
    return pl.pallas_call(empty_kernel, out_shape=(one, one), out_specs=(any_spec, any_spec))()


def times_rows(left, right):
    return lax.dot_general(left, right, (((1,), (1,)), ((), ())), preferred_element_type=jnp.float32)


def body(amp_plus, amp_minus, ints_plus, ints_minus, sym_ij, sym_ab, sym_cd, amp_mask):
    grp, mem = lax.axis_index("grp"), lax.axis_index("mem")
    core, x, y, z = grp % 2, grp // 2, mem // 8, mem % 8
    sign = 1 - 2 * core

    amps = jnp.stack([amp_plus, amp_minus])
    mine = [amps]
    for _ in range(NX - 1):
        mine.append(move(mine[-1], PERM_X))
    other = [move(block, PERM_C) for block in mine]

    flags = ((sym_ij[:, None] == sym_cd[None, :]) & (amp_mask == 1)).astype(jnp.int32)
    plus, minus = empty((768, 4096))
    for t in range(NX):
        tiles = []
        for from_core, from_x in ((core, x - sign * t), (1 - core, x + sign * t)):
            tiles.append(8 * (from_x % NX) + 4 * from_core + jnp.arange(4))
        tiles = jnp.concatenate(tiles)
        step_y = (sign * (y - tiles // 8)) % NY
        step_z = (sign * (z - tiles % 8)) % NZ
        pos = jnp.stack([step_y * NZ + step_z, step_z * NY + step_y]).astype(jnp.int32)
        plus, minus = place(pos, jnp.take(flags, tiles, axis=1), mine[t], other[t], plus, minus)

    zs, ys = [ints_plus], [ints_minus]
    for _ in range(NZ - 1):
        zs.append(move(zs[-1], PERM_Z))
    for _ in range(NY - 1):
        ys.append(move(ys[-1], PERM_Y))
    wide_plus, wide_minus = [jnp.concatenate(zs, axis=1)], [jnp.concatenate(ys, axis=1)]
    for _ in range(NY - 1):
        wide_plus.append(move(wide_plus[-1], PERM_Y))
    for _ in range(NZ - 1):
        wide_minus.append(move(wide_minus[-1], PERM_Z))

    total = None
    for panel, blocks in ((plus, wide_plus), (minus, wide_minus)):
        for k, block in enumerate(blocks):
            width = block.shape[1]
            part = times_rows(panel[:, k * width:(k + 1) * width], block)
            total = part if total is None else total + part
    keep = sym_ij[:, None] == sym_ab[None, :]
    out = (0.5 * total).astype(jnp.bfloat16).reshape(6, BLK, 8, BLK)
    return jnp.where(keep[:, None, :, None], out, jnp.zeros_like(out)).reshape(768, 1024)


def solution(mesh):
    placed = (
        P("mem", "grp"),
        P("mem", "grp"),
        P("grp", "mem"),
        P("grp", "mem"),
        P("mem"),
        P("grp"),
        P(),
        P("mem", None),
    )
    return jax.shard_map(
        body, mesh=mesh, in_specs=placed, out_specs=P("mem", "grp"), check_vma=False
    )
```

```python
import jax
import jax.numpy as jnp
from jax import lax
from jax.experimental import pallas as pl
from jax.experimental.pallas import tpu as pltpu
from jax.sharding import PartitionSpec as P

BLK = 128
AXES = ("grp", "mem")
NX, NY, NZ = 4, 4, 8
HALF = 512
BF16 = jnp.bfloat16


def perm_of(dx, dy, dz, swap=0):
    pairs = []
    for x in range(NX):
        for core in range(2):
            sign = 1 if core == 0 else -1
            for y in range(NY):
                for z in range(NZ):
                    src = (2 * x + core) * 32 + 8 * y + z
                    x2, y2, z2 = (x + sign * dx) % NX, (y + sign * dy) % NY, (z + sign * dz) % NZ
                    core2 = core ^ swap
                    pairs.append((src, (2 * x2 + core2) * 32 + 8 * y2 + z2))
    return pairs


def move(values, dx=0, dy=0, dz=0, swap=0):
    return lax.ppermute(values, AXES, perm_of(dx, dy, dz, swap))


ANY = pl.BlockSpec(memory_space=pl.ANY)
SMEM = pl.BlockSpec(memory_space=pltpu.SMEM)
VMEM = pl.BlockSpec(memory_space=pltpu.VMEM)


def place_kernel(slot_ref, use_ref, mine_ref, other_ref, amps_in, amps_out, sem):
    del amps_in

    def each(act):
        for src, block in enumerate((mine_ref, other_ref)):
            for col in range(4):
                tile = src * 4 + col
                at = pl.multiple_of(slot_ref[tile] * BLK, BLK)
                for row in range(6):
                    @pl.when(use_ref[row, tile] == 1)
                    def _():
                        rows = pl.ds(row * BLK, BLK)
                        act(pltpu.make_async_copy(
                            block.at[:, rows, pl.ds(col * BLK, BLK)], amps_out.at[:, rows, pl.ds(at, BLK)], sem
                        ))

    each(lambda copy: copy.start())
    each(lambda copy: copy.wait())


def place(slots, use, mine, other, amps):
    return pl.pallas_call(
        place_kernel,
        out_shape=jax.ShapeDtypeStruct(amps.shape, amps.dtype),
        in_specs=[SMEM, SMEM, ANY, ANY, ANY],
        out_specs=ANY,
        scratch_shapes=[pltpu.SemaphoreType.DMA],
        input_output_aliases={4: 0},
        cost_estimate=pl.CostEstimate(flops=0, bytes_accessed=4 * 2**20, transcendentals=0),
    )(slots, use, mine, other, amps)


def compact_kernel(slot_ref, use_ref, *refs):
    blocks, out = refs[:-1], refs[-1]
    out[...] = jnp.zeros_like(out)
    cols = blocks[0].shape[2] // BLK
    for b, block in enumerate(blocks):
        for col in range(cols):
            tile = b * cols + col

            @pl.when(use_ref[tile] == 1)
            def _():
                at = pl.multiple_of(slot_ref[tile] * BLK, BLK)
                out[:, :, pl.ds(at, BLK)] = block[:, :, col * BLK:(col + 1) * BLK]


def compact(slots, use, blocks, width):
    rows = blocks[0].shape[1]
    return pl.pallas_call(
        compact_kernel,
        out_shape=jax.ShapeDtypeStruct((2, rows, width), BF16),
        in_specs=[SMEM, SMEM] + [VMEM] * len(blocks),
        out_specs=VMEM,
        compiler_params=pltpu.CompilerParams(vmem_limit_bytes=24 * 2**20),
        cost_estimate=pl.CostEstimate(flops=0, bytes_accessed=4 * 2**20, transcendentals=0),
    )(slots, use, *blocks)


def times_rows(left, right):
    return lax.dot_general(left, right, (((1,), (1,)), ((), ())), preferred_element_type=jnp.float32)


def ladder(slots_n, amp_plus, amp_minus, ints_plus, ints_minus, sym_ij, sym_ab, sym_cd, amp_mask):
    width = slots_n * BLK
    grp, mem = lax.axis_index("grp"), lax.axis_index("mem")
    core, x, y, z = grp % 2, grp // 2, mem // 8, mem % 8
    sign = 1 - 2 * core

    same = sym_cd[:, None] == sym_cd[None, :]
    earlier = jnp.arange(32)[:, None] > jnp.arange(32)[None, :]
    rank = jnp.sum((same & earlier).astype(jnp.int32), axis=1)
    ij_use = ((sym_ij[:, None] == sym_cd[None, :]) & (amp_mask == 1)).astype(jnp.int32)

    ints = jnp.stack([ints_plus, ints_minus])

    def chunk(first, rows, k):
        return lax.dynamic_slice(ints, (0, first + rows * k, 0), (2, rows, BLK))

    deal_a = [chunk(0, BLK, y)]
    deal_b = [chunk(HALF, 64, z)]
    for d in range(1, NY):
        deal_a.append(move(chunk(0, BLK, (y + sign * d) % NY), dy=d))
    for d in range(1, NZ):
        deal_b.append(move(chunk(HALF, 64, (z + sign * d) % NZ), dz=d))

    mine = [jnp.stack([amp_plus, amp_minus])]
    for _ in range(NX - 1):
        mine.append(move(mine[-1], dx=1))
    other = [move(block, swap=1) for block in mine]

    ring_a = [jnp.concatenate(deal_a, axis=2)]
    for _ in range(NZ - 1):
        ring_a.append(move(ring_a[-1], dz=1))
    ring_b = [jnp.concatenate(deal_b, axis=2)]
    for _ in range(NY - 1):
        ring_b.append(move(ring_b[-1], dy=1))
    step_y = (y - sign * jnp.arange(NY)) % NY
    step_z = (z - sign * jnp.arange(NZ)) % NZ
    tiles_a = (8 * step_y[None, :] + step_z[:, None]).reshape(32)
    tiles_b = (8 * step_y[:, None] + step_z[None, :]).reshape(32)
    label_a = sym_ab[y]
    label_b = sym_ab[4 + z // 2]
    rows_a = [compact(rank[tiles_a], (sym_cd[tiles_a] == label_a).astype(jnp.int32), ring_a, width)]
    rows_b = [compact(rank[tiles_b], (sym_cd[tiles_b] == label_b).astype(jnp.int32), ring_b, width)]
    for _ in range(NY - 1):
        rows_a.append(move(rows_a[-1], dy=1))
    for _ in range(NZ - 1):
        rows_b.append(move(rows_b[-1], dz=1))

    amps = jnp.zeros((2, 768, width), BF16)
    for t in range(NX):
        tiles = []
        for from_core, from_x in ((core, x - sign * t), (1 - core, x + sign * t)):
            tiles.append(8 * (from_x % NX) + 4 * from_core + jnp.arange(4))
        tiles = jnp.concatenate(tiles)
        amps = place(rank[tiles], jnp.take(ij_use, tiles, axis=1), mine[t], other[t], amps)

    def product(rows, labels):
        total = times_rows(amps[0], rows[0]) + times_rows(amps[1], rows[1])
        keep = jnp.repeat(sym_ij, BLK)[:, None] == jnp.repeat(labels, BLK)[None, :]
        return jnp.where(keep, 0.5 * total, 0.0).astype(BF16)

    all_b = jnp.zeros((2, HALF, width), BF16)
    for t in range(NZ):
        all_b = lax.dynamic_update_slice(all_b, rows_b[t], (0, 64 * step_z[t], 0))
    out = jnp.zeros((768, 2 * HALF), BF16)
    out = lax.dynamic_update_slice(out, product(all_b, sym_ab[4:]), (0, HALF))
    for t in range(NY):
        part = product(rows_a[t], sym_ab[step_y[t]][None])
        out = lax.dynamic_update_slice(out, part, (0, BLK * step_y[t]))
    return out


SIZES = (18, 20, 24, 32)


def body(*args):
    sym_cd = args[6]
    if len(SIZES) == 1:
        return ladder(SIZES[0], *args)
    ones = jnp.sum(sym_cd)
    need = jnp.maximum(ones, 32 - ones)
    which = sum((need > size).astype(jnp.int32) for size in SIZES[:-1])
    return lax.switch(which, [lambda *a, s=size: ladder(s, *a) for size in SIZES], *args)


def solution(mesh):
    placed = (
        P("mem", "grp"),
        P("mem", "grp"),
        P("grp", "mem"),
        P("grp", "mem"),
        P("mem"),
        P("grp"),
        P(),
        P("mem", None),
    )
    return jax.shard_map(
        body, mesh=mesh, in_specs=placed, out_specs=P("mem", "grp"), check_vma=False
    )
```

```python
import jax
import jax.numpy as jnp
from jax import lax
from jax.experimental import pallas as pl
from jax.experimental.pallas import tpu as pltpu
from jax.sharding import PartitionSpec as P

BLK = 128
AXES = ("grp", "mem")
NX, NY, NZ = 4, 4, 8
BF16 = jnp.bfloat16
F32 = jnp.float32


def perm_of(dx, dy, dz, swap=0):
    pairs = []
    for x in range(NX):
        for core in range(2):
            sign = 1 if core == 0 else -1
            for y in range(NY):
                for z in range(NZ):
                    src = (2 * x + core) * 32 + 8 * y + z
                    x2, y2, z2 = (x + sign * dx) % NX, (y + sign * dy) % NY, (z + sign * dz) % NZ
                    core2 = core ^ swap
                    pairs.append((src, (2 * x2 + core2) * 32 + 8 * y2 + z2))
    return pairs


def move(values, dx=0, dy=0, dz=0, swap=0):
    return lax.ppermute(values, AXES, perm_of(dx, dy, dz, swap))


def after(value, *others):
    return lax.optimization_barrier((value,) + others)[0]


SMEM = pl.BlockSpec(memory_space=pltpu.SMEM)
VMEM = pl.BlockSpec(memory_space=pltpu.VMEM)
ANY = pl.BlockSpec(memory_space=pl.ANY)


def params(mib):
    return pltpu.CompilerParams(vmem_limit_bytes=mib * 2**20)


def cost(flops, moved):
    return pl.CostEstimate(flops=flops, bytes_accessed=moved, transcendentals=0)


def join_kernel(*refs):
    blocks, out = refs[:-1], refs[-1]
    width = blocks[0].shape[1]
    for b, block in enumerate(blocks):
        out[:, b * width:(b + 1) * width] = block[...]


def join(blocks):
    rows, width = blocks[0].shape
    full = width * len(blocks)
    return pl.pallas_call(
        join_kernel,
        out_shape=jax.ShapeDtypeStruct((rows, full), BF16),
        in_specs=[VMEM] * len(blocks),
        out_specs=VMEM,
        compiler_params=params(8),
        cost_estimate=cost(0, 4 * rows * full),
    )(*blocks)


def place_kernel(here_ref, ij_ref, cd_ref, mask_ref, *refs):
    blocks, (plus_out, minus_out) = refs[:-2], refs[-2:]
    sign, x, y, z, core = [here_ref[k] for k in range(5)]
    for b, block in enumerate(blocks):
        way = -sign if b % 2 == 0 else sign
        from_x = (x + way * (b // 2)) & (NX - 1)
        from_core = core if b % 2 == 0 else 1 - core
        step_y = (sign * (y - from_x)) & (NY - 1)
        for col in range(4):
            from_z = 4 * from_core + col
            step_z = (sign * (z - from_z)) & (NZ - 1)
            tile = 8 * from_x + from_z
            label = cd_ref[tile]
            places = ((0, plus_out, step_y * NZ + step_z), (1, minus_out, step_z * NY + step_y))
            for row in range(6):
                on = (ij_ref[row] == label) & (mask_ref[row, tile] == 1)
                rows = slice(row * BLK, (row + 1) * BLK)
                for panel, out, at in places:
                    kept = block[panel, rows, col * BLK:(col + 1) * BLK]
                    out[rows, pl.ds(pl.multiple_of(at * BLK, BLK), BLK)] = jnp.where(on, kept, jnp.zeros_like(kept))


def place(here, sym_ij, sym_cd, amp_mask, blocks):
    one = jax.ShapeDtypeStruct((768, 4096), BF16)
    return pl.pallas_call(
        place_kernel,
        out_shape=(one, one),
        in_specs=[SMEM] * 4 + [VMEM] * len(blocks),
        out_specs=(VMEM, VMEM),
        compiler_params=params(28),
        cost_estimate=cost(0, 25 * 2**20),
    )(here, sym_ij, sym_cd, amp_mask, *blocks)


def dot(left, right):
    return lax.dot_general(left, right, (((1,), (1,)), ((), ())), preferred_element_type=F32)


def product_kernel(places, ij_ref, ab_ref, plus_ref, minus_ref, *refs, first, last):
    blocks, rest = refs[:len(places)], refs[len(places):]
    out = rest[-1]

    def strip(n, carry):
        rows = pl.ds(pl.multiple_of(n * 256, 256), 256)
        total = None if first else rest[0][:, rows]
        for (panel, at), block in zip(places, blocks):
            left = (plus_ref, minus_ref)[panel]
            part = dot(left[:, at:at + block.shape[1]], block[rows, :])
            total = part if total is None else total + part
        if not last:
            out[:, rows] = total
            return carry
        for half in range(2):
            label = ab_ref[2 * n + half]
            for row in range(6):
                tile = total[row * BLK:(row + 1) * BLK, half * BLK:(half + 1) * BLK] * 0.5
                tile = jnp.where(ij_ref[row] == label, tile, jnp.zeros_like(tile))
                where = pl.ds(pl.multiple_of(n * 256 + half * BLK, BLK), BLK)
                out[row * BLK:(row + 1) * BLK, where] = tile.astype(BF16)
        return carry

    lax.fori_loop(0, 4, strip, 0)


def product(sym_ij, sym_ab, plus, minus, terms, so_far=None, last=False):
    first = so_far is None
    blocks = [block for _, _, block in terms]
    places = [(panel, at) for panel, at, _ in terms]
    extra = [] if first else [so_far]
    depth = sum(block.shape[1] for block in blocks)

    def kernel(*refs):
        product_kernel(places, *refs, first=first, last=last)

    return pl.pallas_call(
        kernel,
        out_shape=jax.ShapeDtypeStruct((768, 1024), BF16 if last else F32),
        in_specs=[SMEM] * 2 + [VMEM] * (2 + len(blocks) + len(extra)),
        out_specs=VMEM,
        compiler_params=params(36),
        cost_estimate=cost(2 * 768 * 1024 * depth, 12 * 2**20 + 2 * 1024 * depth),
    )(sym_ij, sym_ab, plus, minus, *blocks, *extra)


def body(amp_plus, amp_minus, ints_plus, ints_minus, sym_ij, sym_ab, sym_cd, amp_mask):
    grp, mem = lax.axis_index("grp"), lax.axis_index("mem")
    core, x, y, z = grp % 2, grp // 2, mem // 8, mem % 8
    here = jnp.stack([1 - 2 * core, x, y, z, core]).astype(jnp.int32)

    def go(value, *waits, **way):
        return move(after(value, *waits) if waits else value, **way)

    t0 = jnp.stack([amp_plus, amp_minus])
    z0, y0 = ints_plus, ints_minus
    z1 = go(z0, dz=1)
    y1, y2, y3 = [go(y0, dy=d) for d in (1, 2, 3)]
    t1 = go(t0, dx=1)
    z2 = go(z1, dz=1)
    z3 = go(z2, dz=1)
    a1, b1 = [[join(pair)] for pair in ((y0, y1), (y2, y3))]
    c1 = [join((z0, z1, z2, z3))]
    a1.append(go(a1[0], z3, dz=1))
    z4 = go(z3, y1, y2, y3, dz=1)
    c1.append(go(c1[0], dy=1))
    s0 = go(t0, z3, swap=1)
    t2 = go(t1, z3, dx=1)
    s1 = go(t1, s0, dx=0, swap=1)
    z5 = go(z4, dz=1)
    b1.append(go(b1[0], a1[1], z4, dz=1))
    z6 = go(z5, dz=1)
    c1.append(go(c1[1], z5, dy=1))
    a1.append(go(a1[1], b1[1], z5, dz=1))
    t3 = go(t2, z5, c1[1], dx=1)
    s2 = go(t2, s1, swap=1)
    z7 = go(z6, dz=1)
    b1.append(go(b1[1], a1[2], z6, dz=1))
    c1.append(go(c1[2], z6, dy=1))
    c2 = [join((z4, z5, z6, z7))]
    c2.append(go(c2[0], dy=1))
    a1.append(go(a1[2], b1[2], z7, dz=1))
    b1.append(go(b1[2], z7, dz=1))
    s3 = go(t3, s2, swap=1)
    a1.append(go(a1[3], dz=1))
    plus, minus = place(here, sym_ij, sym_cd, amp_mask, [t0, s0, t1, s1, t2, s2, t3, s3])
    c2.append(go(c2[1], c1[3], dy=1))
    for k in (4, 5, 6):
        b1.append(go(b1[k - 1], a1[k], dz=1))
        a1.append(go(a1[k], b1[k - 1], dz=1))
        if k == 5:
            c2.append(go(c2[2], dy=1))
    b1.append(go(b1[6], dz=1))

    def term(panel, step, part):
        if panel == 0:
            return panel, 1024 * step + 512 * part, (c1, c2)[part][step]
        return panel, 512 * step + 256 * part, (a1, b1)[part][step]

    early = [term(0, i, 0) for i in range(4)] + [term(0, i, 1) for i in range(2)]
    early += [term(1, t, part) for t in range(4) for part in range(2)]
    late = [term(0, i, 1) for i in (2, 3)] + [term(1, t, part) for t in (4, 5) for part in range(2)]
    rest = [term(1, t, part) for t in (6, 7) for part in range(2)]
    total = product(sym_ij, sym_ab, plus, minus, early)
    total = product(sym_ij, sym_ab, plus, minus, late, total)
    return product(sym_ij, sym_ab, plus, minus, rest, total, last=True)


def solution(mesh):
    placed = (
        P("mem", "grp"),
        P("mem", "grp"),
        P("grp", "mem"),
        P("grp", "mem"),
        P("mem"),
        P("grp"),
        P(),
        P("mem", None),
    )
    return jax.shard_map(
        body, mesh=mesh, in_specs=placed, out_specs=P("mem", "grp"), check_vma=False
    )
```

```python
import jax
import jax.numpy as jnp
from jax import lax
from jax.experimental import pallas as pl
from jax.experimental.pallas import tpu as pltpu
from jax.sharding import PartitionSpec as P

BLK = 128
AXES = ("grp", "mem")
NX, NY, NZ = 4, 4, 8
BF16 = jnp.bfloat16
F32 = jnp.float32


def perm_of(dx, dy, dz, swap=0):
    pairs = []
    for x in range(NX):
        for core in range(2):
            sign = 1 if core == 0 else -1
            for y in range(NY):
                for z in range(NZ):
                    src = (2 * x + core) * 32 + 8 * y + z
                    x2, y2, z2 = (x + sign * dx) % NX, (y + sign * dy) % NY, (z + sign * dz) % NZ
                    core2 = core ^ swap
                    pairs.append((src, (2 * x2 + core2) * 32 + 8 * y2 + z2))
    return pairs


def move(values, dx=0, dy=0, dz=0, swap=0):
    return lax.ppermute(values, AXES, perm_of(dx, dy, dz, swap))


def after(value, *others):
    return lax.optimization_barrier((value,) + others)[0]


SMEM = pl.BlockSpec(memory_space=pltpu.SMEM)
VMEM = pl.BlockSpec(memory_space=pltpu.VMEM)
ANY = pl.BlockSpec(memory_space=pl.ANY)


def params(mib):
    return pltpu.CompilerParams(vmem_limit_bytes=mib * 2**20)


def cost(flops, moved):
    return pl.CostEstimate(flops=flops, bytes_accessed=moved, transcendentals=0)


def join_kernel(*refs):
    blocks, out = refs[:-1], refs[-1]
    width = blocks[0].shape[1]
    for b, block in enumerate(blocks):
        out[:, b * width:(b + 1) * width] = block[...]


def join(blocks):
    rows, width = blocks[0].shape
    full = width * len(blocks)
    return pl.pallas_call(
        join_kernel,
        out_shape=jax.ShapeDtypeStruct((rows, full), BF16),
        in_specs=[VMEM] * len(blocks),
        out_specs=VMEM,
        compiler_params=params(8),
        cost_estimate=cost(0, 4 * rows * full),
    )(*blocks)


def dot(left, right):
    return lax.dot_general(left, right, (((1,), (1,)), ((), ())), preferred_element_type=F32)


def tiles_of(terms):
    return [tile for tiles, _ in terms for tile in tiles]


def early_kernel(terms, parts, here_ref, ij_ref, cd_ref, mask_ref, raw_hbm, *refs):
    n = len(terms)
    ints, outs, (raw, amps, rows_v, sem) = refs[:n], refs[n:-4], refs[-4:]
    copies = [pltpu.make_async_copy(raw_hbm, raw, sem.at[n])]
    at = 0
    for k, block in enumerate(ints):
        width = block.shape[1]
        copies.append(pltpu.make_async_copy(block, rows_v.at[:, pl.ds(at, width)], sem.at[k]))
        at += width
    for copy in copies:
        copy.start()
    sign, y, z = [here_ref[k] for k in range(3)]
    copies[0].wait()
    for target, tiles in zip((amps,) + tuple(outs[1:]), parts):
        for k, (panel, step_y, step_z) in enumerate(tiles):
            tile = 8 * ((y - sign * step_y) & (NY - 1)) + ((z - sign * step_z) & (NZ - 1))
            cols = pl.ds(pl.multiple_of(tile * BLK, BLK), BLK)
            label = cd_ref[tile]
            for row in range(6):
                on = (ij_ref[row] == label) & (mask_ref[row, tile] == 1)
                kept = raw[pl.ds(panel * 768 + row * BLK, BLK), cols]
                target[row * BLK:(row + 1) * BLK, k * BLK:(k + 1) * BLK] = jnp.where(on, kept, jnp.zeros_like(kept))
    for copy in copies[1:]:
        copy.wait()

    def strip(k, carry):
        m = pl.ds(pl.multiple_of((k // 4) * 256, 256), 256)
        c = pl.ds(pl.multiple_of((k % 4) * 256, 256), 256)
        outs[0][m, c] = dot(amps[m, :], rows_v[c, :])
        return carry

    lax.fori_loop(0, 12, strip, 0)


def early(here, sym_ij, sym_cd, amp_mask, raw, terms, later):
    parts = [tiles_of(terms)] + [tiles_of(more) for more in later]
    depth = [len(tiles) * BLK for tiles in parts]

    def kernel(*refs):
        early_kernel(terms, parts, *refs)

    return pl.pallas_call(
        kernel,
        out_shape=[jax.ShapeDtypeStruct((768, 1024), F32)]
        + [jax.ShapeDtypeStruct((768, size), BF16) for size in depth[1:]],
        in_specs=[SMEM] * 4 + [ANY] * (1 + len(terms)),
        out_specs=[VMEM] * len(depth),
        scratch_shapes=[
            pltpu.VMEM((1536, 4096), BF16),
            pltpu.VMEM((768, depth[0]), BF16),
            pltpu.VMEM((1024, depth[0]), BF16),
            pltpu.SemaphoreType.DMA((len(terms) + 1,)),
        ],
        compiler_params=params(46),
        cost_estimate=cost(2 * 768 * 1024 * depth[0], 32 * 2**20),
    )(here, sym_ij, sym_cd, amp_mask, raw, *[block for _, block in terms])


def more_kernel(n, last, ij_ref, ab_ref, amps, total, *refs):
    ints, (out, rows_v, sem) = refs[:n], refs[n:]
    copies = []
    at = 0
    for k, block in enumerate(ints):
        width = block.shape[1]
        copies.append(pltpu.make_async_copy(block, rows_v.at[:, pl.ds(at, width)], sem.at[k]))
        at += width
    for copy in copies:
        copy.start()
    for copy in copies:
        copy.wait()

    def strip(k, carry):
        m = pl.ds(pl.multiple_of((k // 4) * 256, 256), 256)
        c = pl.ds(pl.multiple_of((k % 4) * 256, 256), 256)
        value = total[m, c] + dot(amps[m, :], rows_v[c, :])
        if not last:
            out[m, c] = value
            return carry
        for i in range(2):
            for j in range(2):
                tile = value[i * BLK:(i + 1) * BLK, j * BLK:(j + 1) * BLK] * 0.5
                on = ij_ref[2 * (k // 4) + i] == ab_ref[2 * (k % 4) + j]
                where = (
                    pl.ds(pl.multiple_of((k // 4) * 256 + i * BLK, BLK), BLK),
                    pl.ds(pl.multiple_of((k % 4) * 256 + j * BLK, BLK), BLK),
                )
                out[where] = jnp.where(on, tile, jnp.zeros_like(tile)).astype(BF16)
        return carry

    lax.fori_loop(0, 12, strip, 0)


def more(sym_ij, sym_ab, amps, total, terms, last):
    depth = amps.shape[1]

    def kernel(*refs):
        more_kernel(len(terms), last, *refs)

    return pl.pallas_call(
        kernel,
        out_shape=jax.ShapeDtypeStruct((768, 1024), BF16 if last else F32),
        in_specs=[SMEM] * 2 + [VMEM] * 2 + [ANY] * len(terms),
        out_specs=VMEM,
        scratch_shapes=[pltpu.VMEM((1024, depth), BF16), pltpu.SemaphoreType.DMA((len(terms),))],
        compiler_params=params(20),
        cost_estimate=cost(2 * 768 * 1024 * depth, 8 * 2**20 + 3584 * depth),
    )(sym_ij, sym_ab, amps, total, *[block for _, block in terms])


def body(amp_plus, amp_minus, ints_plus, ints_minus, sym_ij, sym_ab, sym_cd, amp_mask):
    grp, mem = lax.axis_index("grp"), lax.axis_index("mem")
    here = jnp.stack([1 - 2 * (grp % 2), mem // 8, mem % 8]).astype(jnp.int32)

    def go(value, *waits, **way):
        return move(after(value, *waits) if waits else value, **way)

    raw = lax.all_gather(jnp.concatenate([amp_plus, amp_minus], axis=0), "grp", axis=1, tiled=True)

    z0, y0 = ints_plus, ints_minus
    z1, y1 = go(z0, dz=1), go(y0, dy=1)
    z2, y2 = go(z1, y1, dz=1), go(y1, z1, dy=1)
    z3, y3 = go(z2, y2, dz=1), go(y2, z2, dy=1)
    z4 = go(z3, y3, dz=1)
    a, b, c = [join((y0, y1))], [join((y2, y3))], [join((z0, z1, z2, z3))]
    a.append(go(a[0], dz=1))
    c.append(go(c[0], dy=1))
    b.append(go(b[0], dz=1))
    z5 = go(z4, dz=1)
    a.append(go(a[1], z4, dz=1))
    b.append(go(b[1], a[1], dz=1))
    d = [join((z4, z5))]
    z6 = go(z5, b[1], dz=1)
    c.append(go(c[1], b[1], dy=1))
    d.append(go(d[0], dy=1))
    a.append(go(a[2], z5, dz=1))
    b.append(go(b[2], a[2], dz=1))
    z7 = go(z6, b[2], dz=1)
    e = [join((z6, z7))]
    c.append(go(c[2], b[2], dy=1))
    d.append(go(d[1], b[2], dy=1))
    a.append(go(a[3], z6, dz=1))
    b.append(go(b[3], a[3], dz=1))
    e.append(go(e[0], b[3], dy=1))
    d.append(go(d[2], b[3], dy=1))
    a.append(go(a[4], z7, dz=1))
    b.append(go(b[4], a[4], dz=1))
    a.append(go(a[5], b[4], dz=1))
    e.append(go(e[1], a[5], dy=1))
    b.append(go(b[5], a[5], dz=1))
    a.append(go(a[6], b[5], dz=1))
    e.append(go(e[2], a[6], dy=1))
    b.append(go(b[6], a[6], dz=1))

    def plus(blocks, i, first):
        count = blocks[i].shape[1] // BLK
        return [(0, i, first + k) for k in range(count)], blocks[i]

    def minus(blocks, t, first):
        return [(1, first + k, t) for k in range(2)], blocks[t]

    now = [plus(c, i, 0) for i in range(4)] + [plus(d, i, 4) for i in range(2)] + [plus(e, 0, 6)]
    now += [term for t in range(5) for term in (minus(a, t, 0), minus(b, t, 2))]
    soon = [plus(d, 2, 4), plus(d, 3, 4), plus(e, 1, 6)]
    soon += [term for t in (5, 6) for term in (minus(a, t, 0), minus(b, t, 2))]
    rest = [plus(e, 2, 6), plus(e, 3, 6), minus(a, 7, 0), minus(b, 7, 2)]
    total, amps_soon, amps_rest = early(here, sym_ij, sym_cd, amp_mask, raw, now, (soon, rest))
    total = more(sym_ij, sym_ab, amps_soon, total, soon, False)
    return more(sym_ij, sym_ab, amps_rest, total, rest, True)


def solution(mesh):
    placed = (
        P("mem", "grp"),
        P("mem", "grp"),
        P("grp", "mem"),
        P("grp", "mem"),
        P("mem"),
        P("grp"),
        P(),
        P("mem", None),
    )
    return jax.shard_map(
        body, mesh=mesh, in_specs=placed, out_specs=P("mem", "grp"), check_vma=False
    )
```

```python
import jax
import jax.numpy as jnp
from jax import lax
from jax.experimental import pallas as pl
from jax.experimental.pallas import tpu as pltpu
from jax.sharding import PartitionSpec as P

BLK = 128
AXES = ("grp", "mem")
NX, NY, NZ = 4, 4, 8
BF16 = jnp.bfloat16
F32 = jnp.float32


def perm_of(dx, dy, dz, swap=0):
    pairs = []
    for x in range(NX):
        for core in range(2):
            sign = 1 if core == 0 else -1
            for y in range(NY):
                for z in range(NZ):
                    src = (2 * x + core) * 32 + 8 * y + z
                    x2, y2, z2 = (x + sign * dx) % NX, (y + sign * dy) % NY, (z + sign * dz) % NZ
                    core2 = core ^ swap
                    pairs.append((src, (2 * x2 + core2) * 32 + 8 * y2 + z2))
    return pairs


def move(values, dx=0, dy=0, dz=0, swap=0):
    return lax.ppermute(values, AXES, perm_of(dx, dy, dz, swap))


def after(value, *others):
    return lax.optimization_barrier((value,) + others)[0]


SMEM = pl.BlockSpec(memory_space=pltpu.SMEM)
VMEM = pl.BlockSpec(memory_space=pltpu.VMEM)
HBM = pl.BlockSpec(memory_space=pltpu.HBM)


def params(mib):
    return pltpu.CompilerParams(vmem_limit_bytes=mib * 2**20)


def cost(flops, moved):
    return pl.CostEstimate(flops=flops, bytes_accessed=moved, transcendentals=0)


def join_kernel(*refs):
    blocks, out = refs[:-1], refs[-1]
    width = blocks[0].shape[1]
    for b, block in enumerate(blocks):
        out[:, b * width:(b + 1) * width] = block[...]


def join(blocks):
    rows, width = blocks[0].shape
    full = width * len(blocks)
    return pl.pallas_call(
        join_kernel,
        out_shape=jax.ShapeDtypeStruct((rows, full), BF16),
        in_specs=[VMEM] * len(blocks),
        out_specs=VMEM,
        compiler_params=params(8),
        cost_estimate=cost(0, 4 * rows * full),
    )(*blocks)


def dot(left, right):
    return lax.dot_general(left, right, (((1,), (1,)), ((), ())), preferred_element_type=F32)


def tiles_of(terms):
    return [tile for tiles, _ in terms for tile in tiles]


def mask_kernel(parts, here_ref, ij_ref, cd_ref, mask_ref, raw_hbm, *refs):
    outs, raw, laid, sem = refs[:len(parts)], refs[-2 - len(parts)], refs[-1 - len(parts):-1], refs[-1]
    fetch = pltpu.make_async_copy(raw_hbm, raw, sem.at[len(parts)])
    fetch.start()
    sign, y, z = [here_ref[k] for k in range(3)]
    fetch.wait()
    copies = []
    for p, (target, tiles) in enumerate(zip(laid, parts)):
        for k, (panel, step_y, step_z) in enumerate(tiles):
            tile = 8 * ((y - sign * step_y) & (NY - 1)) + ((z - sign * step_z) & (NZ - 1))
            cols = pl.ds(pl.multiple_of(tile * BLK, BLK), BLK)
            label = cd_ref[tile]
            for row in range(6):
                on = (ij_ref[row] == label) & (mask_ref[row, tile] == 1)
                kept = raw[pl.ds(panel * 768 + row * BLK, BLK), cols]
                target[row * BLK:(row + 1) * BLK, k * BLK:(k + 1) * BLK] = jnp.where(on, kept, jnp.zeros_like(kept))
        copies.append(pltpu.make_async_copy(target, outs[p], sem.at[p]))
        copies[-1].start()
    for copy in copies:
        copy.wait()


def mask(here, sym_ij, sym_cd, amp_mask, raw, groups):
    parts = [tiles_of(terms) for terms in groups]
    shapes = [(768, len(tiles) * BLK) for tiles in parts]

    def kernel(*refs):
        mask_kernel(parts, *refs)

    return pl.pallas_call(
        kernel,
        out_shape=[jax.ShapeDtypeStruct(shape, BF16) for shape in shapes],
        in_specs=[SMEM] * 4 + [HBM],
        out_specs=[HBM] * len(shapes),
        scratch_shapes=[pltpu.VMEM((1536, 4096), BF16)]
        + [pltpu.VMEM(shape, BF16) for shape in shapes]
        + [pltpu.SemaphoreType.DMA((len(shapes) + 1,))],
        compiler_params=params(60),
        cost_estimate=cost(0, 25 * 2**20),
    )(here, sym_ij, sym_cd, amp_mask, raw)


def product_kernel(n, first, last, ij_ref, ab_ref, amps_hbm, *refs):
    ints, refs = refs[:n], refs[n:]
    if first:
        out, amps, rows_v, sem = refs
    else:
        total_hbm, out, amps, rows_v, sem, total = refs

    def fetch(c):
        rows = pl.ds(pl.multiple_of(c * 256, 256), 256)
        copies, at = [], 0
        for k, block in enumerate(ints):
            width = block.shape[1]
            copies.append(pltpu.make_async_copy(block.at[rows, :], rows_v.at[rows, pl.ds(at, width)], sem.at[c, k]))
            at += width
        if not first:
            copies.append(pltpu.make_async_copy(total_hbm.at[:, rows], total.at[:, rows], sem.at[c, n]))
        return copies

    whole = pltpu.make_async_copy(amps_hbm, amps, sem.at[4, 0])
    whole.start()
    for c in range(4):
        for copy in fetch(c):
            copy.start()
    whole.wait()

    def strip(c, carry):
        for copy in fetch(c):
            copy.wait()
        cols = pl.ds(pl.multiple_of(c * 256, 256), 256)

        def part(m, carry):
            rows = pl.ds(pl.multiple_of(m * 256, 256), 256)
            value = dot(amps[rows, :], rows_v[cols, :])
            if not first:
                value = value + total[rows, cols]
            if not last:
                out[rows, cols] = value
                return carry
            for i in range(2):
                for j in range(2):
                    tile = value[i * BLK:(i + 1) * BLK, j * BLK:(j + 1) * BLK] * 0.5
                    on = ij_ref[2 * m + i] == ab_ref[2 * c + j]
                    where = (
                        pl.ds(pl.multiple_of(m * 256 + i * BLK, BLK), BLK),
                        pl.ds(pl.multiple_of(c * 256 + j * BLK, BLK), BLK),
                    )
                    out[where] = jnp.where(on, tile, jnp.zeros_like(tile)).astype(BF16)
            return carry

        return lax.fori_loop(0, 3, part, carry)

    lax.fori_loop(0, 4, strip, 0)


def product(sym_ij, sym_ab, amps, terms, total=None, last=False):
    depth = amps.shape[1]
    first = total is None
    n = len(terms)

    def kernel(*refs):
        product_kernel(n, first, last, *refs)

    scratch = [
        pltpu.VMEM((768, depth), BF16), pltpu.VMEM((1024, depth), BF16), pltpu.SemaphoreType.DMA((5, n + 1))
    ]
    return pl.pallas_call(
        kernel,
        out_shape=jax.ShapeDtypeStruct((768, 1024), BF16 if last else F32),
        in_specs=[SMEM] * 2 + [HBM] * (1 + n + (not first)),
        out_specs=VMEM,
        scratch_shapes=scratch + ([] if first else [pltpu.VMEM((768, 1024), F32)]),
        compiler_params=params(60),
        cost_estimate=cost(2 * 768 * 1024 * depth, 8 * 2**20 + 3584 * depth),
    )(sym_ij, sym_ab, amps, *[block for _, block in terms], *([] if first else [total]))


def body(amp_plus, amp_minus, ints_plus, ints_minus, sym_ij, sym_ab, sym_cd, amp_mask):
    grp, mem = lax.axis_index("grp"), lax.axis_index("mem")
    here = jnp.stack([1 - 2 * (grp % 2), mem // 8, mem % 8]).astype(jnp.int32)

    def go(value, *waits, **way):
        return move(after(value, *waits) if waits else value, **way)

    raw = lax.all_gather(jnp.concatenate([amp_plus, amp_minus], axis=0), "grp", axis=1, tiled=True)

    z0, y0 = ints_plus, ints_minus
    z1, y1 = go(z0, dz=1), go(y0, dy=1)
    z2, y2 = go(z1, y1, dz=1), go(y1, z1, dy=1)
    z3, y3 = go(z2, y2, dz=1), go(y2, z2, dy=1)
    a, b, c = [join((y0, y1))], [join((y2, y3))], [join((z0, z1, z2, z3))]
    z4 = go(z3, y3, a[0], b[0], c[0], dz=1)
    a.append(go(a[0], dz=1))
    b.append(go(b[0], dz=1))
    c.append(go(c[0], dy=1))
    z5 = go(z4, a[1], dz=1)
    a.append(go(a[1], z4, dz=1))
    b.append(go(b[1], a[1], dz=1))
    d = [join((z4, z5))]
    c.append(go(c[1], b[1], dy=1))
    z6 = go(z5, a[2], dz=1)
    a.append(go(a[2], z5, dz=1))
    d.append(go(d[0], b[1], dy=1))
    b.append(go(b[2], a[2], dz=1))
    z7 = go(z6, a[3], dz=1)
    c.append(go(c[2], b[2], dy=1))
    a.append(go(a[3], z6, dz=1))
    d.append(go(d[1], b[2], dy=1))
    b.append(go(b[3], a[3], dz=1))
    e = [join((z6, z7))]
    d.append(go(d[2], b[3], dy=1))
    e.append(go(e[0], a[4], dy=1))

    def plus(blocks, i, first):
        count = blocks[i].shape[1] // BLK
        return [(0, i, first + k) for k in range(count)], blocks[i]

    def minus(blocks, t, first):
        return [(1, first + k, t) for k in range(2)], blocks[t]

    a.append(go(a[4], z7, dz=1))
    b.append(go(b[4], a[4], dz=1))
    now = [plus(c, i, 0) for i in range(4)] + [plus(d, i, 4) for i in range(4)] + [plus(e, 0, 6)]
    now += [term for t in range(5) for term in (minus(a, t, 0), minus(b, t, 2))]
    groups = [
        now,
        [([(0, i, 6), (0, i, 7)], None) for i in (1, 2)]
        + [([(1, first, t), (1, first + 1, t)], None) for t in (5, 6) for first in (0, 2)],
        [([(0, 3, 6), (0, 3, 7)], None)] + [([(1, first, 7), (1, first + 1, 7)], None) for first in (0, 2)],
    ]
    amps = mask(here, sym_ij, sym_cd, amp_mask, raw, groups)
    a.append(go(a[5], b[4], amps[0], dz=1))
    e.append(go(e[1], a[5], dy=1))
    b.append(go(b[5], a[5], dz=1))
    total = product(sym_ij, sym_ab, amps[0], now)
    a.append(go(a[6], b[5], total, dz=1))
    e.append(go(e[2], a[6], dy=1))
    b.append(go(b[6], a[6], dz=1))
    soon = [plus(e, 1, 6), plus(e, 2, 6)]
    soon += [term for t in (5, 6) for term in (minus(a, t, 0), minus(b, t, 2))]
    rest = [plus(e, 3, 6), minus(a, 7, 0), minus(b, 7, 2)]
    total = product(sym_ij, sym_ab, amps[1], soon, total)
    return product(sym_ij, sym_ab, amps[2], rest, total, True)


def solution(mesh):
    placed = (
        P("mem", "grp"),
        P("mem", "grp"),
        P("grp", "mem"),
        P("grp", "mem"),
        P("mem"),
        P("grp"),
        P(),
        P("mem", None),
    )
    return jax.shard_map(
        body, mesh=mesh, in_specs=placed, out_specs=P("mem", "grp"), check_vma=False
    )
```

```python
import jax
import jax.numpy as jnp
from jax import lax
from jax.experimental import pallas as pl
from jax.experimental.pallas import tpu as pltpu
from jax.sharding import PartitionSpec as P

BLK = 128
NY, NZ = 4, 8
HALF = 512
BF16 = jnp.bfloat16
F32 = jnp.float32


def perm_of(dy, dz):
    return [
        (8 * y + z, 8 * ((y + dy) % NY) + (z + dz) % NZ) for y in range(NY) for z in range(NZ)
    ]


def move(values, dy=0, dz=0):
    return lax.ppermute(values, "mem", perm_of(dy, dz))


def after(value, *others):
    return lax.optimization_barrier((value,) + others)[0]


SMEM = pl.BlockSpec(memory_space=pltpu.SMEM)
VMEM = pl.BlockSpec(memory_space=pltpu.VMEM)
HBM = pl.BlockSpec(memory_space=pltpu.HBM)


def params(mib):
    return pltpu.CompilerParams(vmem_limit_bytes=mib * 2**20)


def cost(flops, moved):
    return pl.CostEstimate(flops=flops, bytes_accessed=moved, transcendentals=0)


def join_kernel(blocks, *refs):
    out, at, k = refs[-1], 0, 0
    for block in blocks:
        width = block[0].shape[1]
        if len(block) == 1:
            out[:, at:at + width] = refs[k][...]
        else:
            out[:HALF, at:at + width] = refs[k][...]
            out[HALF:, at:at + width] = refs[k + 1][...]
        at += width
        k += len(block)


def join(blocks):
    arrays = [array for block in blocks for array in block]
    full = sum(block[0].shape[1] for block in blocks)

    def kernel(*refs):
        join_kernel(blocks, *refs)

    return pl.pallas_call(
        kernel,
        out_shape=jax.ShapeDtypeStruct((2 * HALF, full), BF16),
        in_specs=[VMEM] * len(arrays),
        out_specs=VMEM,
        compiler_params=params(8),
        cost_estimate=cost(0, 8 * HALF * full),
    )(*arrays)


def dot(left, right):
    return lax.dot_general(left, right, (((1,), (1,)), ((), ())), preferred_element_type=F32)


def tiles_of(terms):
    return [tile for tiles, _ in terms for tile in tiles]


def mask_kernel(parts, here_ref, ij_ref, cd_ref, mask_ref, raw_hbm, *refs):
    outs, raw, laid, sem = refs[:len(parts)], refs[-2 - len(parts)], refs[-1 - len(parts):-1], refs[-1]
    fetch = pltpu.make_async_copy(raw_hbm, raw, sem.at[len(parts)])
    fetch.start()
    y, z = here_ref[0], here_ref[1]
    fetch.wait()
    copies = []
    for p, (target, tiles) in enumerate(zip(laid, parts)):
        for k, (panel, off_y, off_z) in enumerate(tiles):
            tile = 8 * ((y + off_y) & (NY - 1)) + ((z + off_z) & (NZ - 1))
            cols = pl.ds(pl.multiple_of(tile * BLK, BLK), BLK)
            label = cd_ref[tile]
            for row in range(6):
                on = (ij_ref[row] == label) & (mask_ref[row, tile] == 1)
                kept = raw[pl.ds(panel * 768 + row * BLK, BLK), cols]
                target[row * BLK:(row + 1) * BLK, k * BLK:(k + 1) * BLK] = jnp.where(on, kept, jnp.zeros_like(kept))
        copies.append(pltpu.make_async_copy(target, outs[p], sem.at[p]))
        copies[-1].start()
    for copy in copies:
        copy.wait()


def mask(here, sym_ij, sym_cd, amp_mask, raw, groups):
    parts = [tiles_of(terms) for terms in groups]
    shapes = [(768, len(tiles) * BLK) for tiles in parts]

    def kernel(*refs):
        mask_kernel(parts, *refs)

    return pl.pallas_call(
        kernel,
        out_shape=[jax.ShapeDtypeStruct(shape, BF16) for shape in shapes],
        in_specs=[SMEM] * 4 + [HBM],
        out_specs=[HBM] * len(shapes),
        scratch_shapes=[pltpu.VMEM((1536, 4096), BF16)]
        + [pltpu.VMEM(shape, BF16) for shape in shapes]
        + [pltpu.SemaphoreType.DMA((len(shapes) + 1,))],
        compiler_params=params(60),
        cost_estimate=cost(0, 25 * 2**20),
    )(here, sym_ij, sym_cd, amp_mask, raw)


def product_kernel(sizes, first, last, ij_ref, ab_ref, amps_hbm, *refs):
    n = sum(sizes)
    ints, refs = refs[:n], refs[n:]
    if first:
        out, amps, rows_v, sem = refs
    else:
        total_hbm, out, amps, rows_v, sem, total = refs

    def fetch(c, act):
        rows = pl.ds(pl.multiple_of(c * 256, 256), 256)
        at, k = 0, 0
        for b, size in enumerate(sizes):
            width = ints[k].shape[1]
            to = rows_v.at[rows, pl.ds(at, width)]
            if size == 1:
                act(pltpu.make_async_copy(ints[k].at[rows, :], to, sem.at[c, b]))
            else:
                part = pl.ds(pl.multiple_of((c & 1) * 256, 256), 256)

                @pl.when(c < 2)
                def _():
                    act(pltpu.make_async_copy(ints[k].at[part, :], to, sem.at[c, b]))

                @pl.when(c >= 2)
                def _():
                    act(pltpu.make_async_copy(ints[k + 1].at[part, :], to, sem.at[c, b]))
            at += width
            k += size
        if not first:
            act(pltpu.make_async_copy(total_hbm.at[:, rows], total.at[:, rows], sem.at[c, len(sizes)]))

    whole = pltpu.make_async_copy(amps_hbm, amps, sem.at[4, 0])
    whole.start()
    for c in range(4):
        fetch(jnp.int32(c), lambda copy: copy.start())
    whole.wait()

    def strip(c, carry):
        fetch(c, lambda copy: copy.wait())
        cols = pl.ds(pl.multiple_of(c * 256, 256), 256)

        def part(m, carry):
            rows = pl.ds(pl.multiple_of(m * 256, 256), 256)
            value = dot(amps[rows, :], rows_v[cols, :])
            if not first:
                value = value + total[rows, cols]
            if not last:
                out[rows, cols] = value
                return carry
            for i in range(2):
                for j in range(2):
                    tile = value[i * BLK:(i + 1) * BLK, j * BLK:(j + 1) * BLK] * 0.5
                    on = ij_ref[2 * m + i] == ab_ref[2 * c + j]
                    where = (
                        pl.ds(pl.multiple_of(m * 256 + i * BLK, BLK), BLK),
                        pl.ds(pl.multiple_of(c * 256 + j * BLK, BLK), BLK),
                    )
                    out[where] = jnp.where(on, tile, jnp.zeros_like(tile)).astype(BF16)
            return carry

        return lax.fori_loop(0, 3, part, carry)

    lax.fori_loop(0, 4, strip, 0)


def product(sym_ij, sym_ab, amps, terms, total=None, last=False):
    depth = amps.shape[1]
    first = total is None
    sizes = [len(block) for _, block in terms]
    n = sum(sizes)

    def kernel(*refs):
        product_kernel(sizes, first, last, *refs)

    scratch = [
        pltpu.VMEM((768, depth), BF16), pltpu.VMEM((1024, depth), BF16), pltpu.SemaphoreType.DMA((5, len(sizes) + 1))
    ]
    return pl.pallas_call(
        kernel,
        out_shape=jax.ShapeDtypeStruct((768, 1024), BF16 if last else F32),
        in_specs=[SMEM] * 2 + [HBM] * (1 + n + (not first)),
        out_specs=VMEM,
        scratch_shapes=scratch + ([] if first else [pltpu.VMEM((768, 1024), F32)]),
        compiler_params=params(60),
        cost_estimate=cost(2 * 768 * 1024 * depth, 8 * 2**20 + 3584 * depth),
    )(sym_ij, sym_ab, amps, *[array for _, block in terms for array in block], *([] if first else [total]))


def body(amp_plus, amp_minus, ints_plus, ints_minus, sym_ij, sym_ab, sym_cd, amp_mask):
    mem = lax.axis_index("mem")
    here = jnp.stack([mem // NZ, mem % NZ]).astype(jnp.int32)

    def go(value, *waits, **way):
        return move(after(value, *waits) if waits else value, **way)

    raw = lax.all_gather(jnp.concatenate([amp_plus, amp_minus], axis=0), "grp", axis=1, tiled=True)

    z0, y0 = ints_plus, ints_minus
    zu, zd, yu, yd = [go(z0, dz=1)], [go(z0, dz=-1)], [go(y0, dy=1)], [go(y0, dy=-1)]
    ones = (zu[0], zd[0], yu[0], yd[0])
    zu.append(go(zu[0], *ones, dz=1))
    zd.append(go(zd[0], *ones, dz=-1))
    y2 = (go(yu[0][:HALF], *ones, dy=1), go(yd[0][HALF:], *ones, dy=-1))
    twos = (zu[1], zd[1]) + y2
    zu.append(go(zu[1], *twos, dz=1))
    zd.append(go(zd[1], *twos, dz=-1))
    c0 = join([(z0,), (zu[0],), (zd[0],), (zu[1],), (zd[1],)])
    c1 = (go(c0, *twos, dy=1), go(c0, *twos, dy=-1))
    w0 = join([(y0,), (yu[0],), (yd[0],), y2])
    threes = (zu[2], zd[2])
    z4 = (go(zu[2][:HALF], *threes, dz=1), go(zd[2][HALF:], *threes, dz=-1))
    d0 = join([(zu[2],), (zd[2],), z4])
    wu, wd = [go(w0, *z4, dz=1)], [go(w0, *z4, dz=-1)]
    c2 = (go(c1[0][:HALF], *c1, dy=1), go(c1[1][HALF:], *c1, dy=-1))
    wu.append(go(wu[0], wd[0], dz=1))
    wd.append(go(wd[0], wu[0], dz=-1))
    d1 = (go(d0, *c2, dy=1), go(d0, *c2, dy=-1))
    wu.append(go(wu[1], wd[1], dz=1))
    wd.append(go(wd[1], wu[1], dz=-1))

    def plus(offs, y, block):
        return [(0, y, z) for z in offs], block

    def minus(z, block):
        return [(1, y, z) for y in (0, -1, 1, 2)], block

    near, far = (0, -1, 1, -2, 2), (-3, 3, 4)
    now = [plus(near, 0, (c0,)), plus(near, -1, c1[:1]), plus(near, 1, c1[1:]), plus(near, 2, c2)]
    now += [minus(0, (w0,)), minus(-1, (wu[0],)), minus(1, (wd[0],))]
    far4 = [(0, y, z) for y in (0, -1, 1, 2) for z in far]
    tiles = [(far4, None)] + [minus(z, None) for z in (-2, 2, -3, 3)]
    amps = mask(here, sym_ij, sym_cd, amp_mask, raw, (now, tiles, [minus(4, None)]))
    total = product(sym_ij, sym_ab, amps[0], now)
    d2 = (go(d1[0][:HALF], *d1, total, dy=1), go(d1[1][HALF:], *d1, total, dy=-1))
    soon = [plus(far, 0, (d0,)), plus(far, -1, d1[:1]), plus(far, 1, d1[1:]), plus(far, 2, d2)]
    soon += [minus(-2, (wu[1],)), minus(2, (wd[1],)), minus(-3, (wu[2],)), minus(3, (wd[2],))]
    w4 = (go(wu[2][:HALF], wd[2], *d2, dz=1), go(wd[2][HALF:], wu[2], *d2, dz=-1))
    total = product(sym_ij, sym_ab, amps[1], soon, total)
    return product(sym_ij, sym_ab, amps[2], [minus(4, w4)], total, True)


def solution(mesh):
    placed = (
        P("mem", "grp"),
        P("mem", "grp"),
        P("grp", "mem"),
        P("grp", "mem"),
        P("mem"),
        P("grp"),
        P(),
        P("mem", None),
    )
    return jax.shard_map(
        body, mesh=mesh, in_specs=placed, out_specs=P("mem", "grp"), check_vma=False
    )
```

```python
import jax
import jax.numpy as jnp
from jax import lax
from jax.experimental import pallas as pl
from jax.experimental.pallas import tpu as pltpu
from jax.sharding import PartitionSpec as P

BLK = 128
NY, NZ = 4, 8
HALF = 512
BF16 = jnp.bfloat16
F32 = jnp.float32


def perm_of(dy, dz):
    return [
        (8 * y + z, 8 * ((y + dy) % NY) + (z + dz) % NZ) for y in range(NY) for z in range(NZ)
    ]


def move(values, dy=0, dz=0):
    return lax.ppermute(values, "mem", perm_of(dy, dz))


def after(value, *others):
    return lax.optimization_barrier((value,) + others)[0]


SMEM = pl.BlockSpec(memory_space=pltpu.SMEM)
VMEM = pl.BlockSpec(memory_space=pltpu.VMEM)
HBM = pl.BlockSpec(memory_space=pltpu.HBM)


def params(mib):
    return pltpu.CompilerParams(vmem_limit_bytes=mib * 2**20)


def cost(flops, moved):
    return pl.CostEstimate(flops=flops, bytes_accessed=moved, transcendentals=0)


def join_kernel(blocks, *refs):
    out, at, k = refs[-1], 0, 0
    for block in blocks:
        width = block[0].shape[1]
        if len(block) == 1:
            out[:, at:at + width] = refs[k][...]
        else:
            out[:HALF, at:at + width] = refs[k][...]
            out[HALF:, at:at + width] = refs[k + 1][...]
        at += width
        k += len(block)


def join(blocks):
    arrays = [array for block in blocks for array in block]
    full = sum(block[0].shape[1] for block in blocks)

    def kernel(*refs):
        join_kernel(blocks, *refs)

    return pl.pallas_call(
        kernel,
        out_shape=jax.ShapeDtypeStruct((2 * HALF, full), BF16),
        in_specs=[VMEM] * len(arrays),
        out_specs=VMEM,
        compiler_params=params(8),
        cost_estimate=cost(0, 8 * HALF * full),
    )(*arrays)


def dot(left, right):
    return lax.dot_general(left, right, (((1,), (1,)), ((), ())), preferred_element_type=F32)


def tiles_of(terms):
    return [tile for tiles, _ in terms for tile in tiles]


def mask_kernel(parts, here_ref, ij_ref, cd_ref, mask_ref, raw_hbm, *refs):
    outs, raw, laid, sem = refs[:len(parts)], refs[-2 - len(parts)], refs[-1 - len(parts):-1], refs[-1]
    fetch = pltpu.make_async_copy(raw_hbm, raw, sem.at[len(parts)])
    fetch.start()
    y, z = here_ref[0], here_ref[1]
    fetch.wait()
    copies = []
    for p, (target, tiles) in enumerate(zip(laid, parts)):
        for k, (panel, off_y, off_z) in enumerate(tiles):
            tile = 8 * ((y + off_y) & (NY - 1)) + ((z + off_z) & (NZ - 1))
            cols = pl.ds(pl.multiple_of(tile * BLK, BLK), BLK)
            label = cd_ref[tile]
            for row in range(6):
                on = (ij_ref[row] == label) & (mask_ref[row, tile] == 1)
                kept = raw[pl.ds(panel * 768 + row * BLK, BLK), cols]
                target[row * BLK:(row + 1) * BLK, k * BLK:(k + 1) * BLK] = jnp.where(on, kept, jnp.zeros_like(kept))
        copies.append(pltpu.make_async_copy(target, outs[p], sem.at[p]))
        copies[-1].start()
    for copy in copies:
        copy.wait()


def mask(here, sym_ij, sym_cd, amp_mask, raw, groups):
    parts = [tiles_of(terms) for terms in groups]
    shapes = [(768, len(tiles) * BLK) for tiles in parts]

    def kernel(*refs):
        mask_kernel(parts, *refs)

    return pl.pallas_call(
        kernel,
        out_shape=[jax.ShapeDtypeStruct(shape, BF16) for shape in shapes],
        in_specs=[SMEM] * 4 + [HBM],
        out_specs=[HBM] * len(shapes),
        scratch_shapes=[pltpu.VMEM((1536, 4096), BF16)]
        + [pltpu.VMEM(shape, BF16) for shape in shapes]
        + [pltpu.SemaphoreType.DMA((len(shapes) + 1,))],
        compiler_params=params(60),
        cost_estimate=cost(0, 25 * 2**20),
    )(here, sym_ij, sym_cd, amp_mask, raw)


def product_kernel(sizes, first, last, ij_ref, ab_ref, amps_hbm, *refs):
    n = sum(sizes)
    ints, refs = refs[:n], refs[n:]
    if first:
        out, amps, rows_v, sem = refs
    else:
        total_hbm, out, amps, rows_v, sem, total = refs

    def fetch(c, act):
        rows = pl.ds(pl.multiple_of(c * 256, 256), 256)
        at, k = 0, 0
        for b, size in enumerate(sizes):
            width = ints[k].shape[1]
            to = rows_v.at[rows, pl.ds(at, width)]
            if size == 1:
                act(pltpu.make_async_copy(ints[k].at[rows, :], to, sem.at[c, b]))
            else:
                part = pl.ds(pl.multiple_of((c & 1) * 256, 256), 256)

                @pl.when(c < 2)
                def _():
                    act(pltpu.make_async_copy(ints[k].at[part, :], to, sem.at[c, b]))

                @pl.when(c >= 2)
                def _():
                    act(pltpu.make_async_copy(ints[k + 1].at[part, :], to, sem.at[c, b]))
            at += width
            k += size
        if not first:
            act(pltpu.make_async_copy(total_hbm.at[:, rows], total.at[:, rows], sem.at[c, len(sizes)]))

    whole = pltpu.make_async_copy(amps_hbm, amps, sem.at[4, 0])
    whole.start()
    for c in range(4):
        fetch(jnp.int32(c), lambda copy: copy.start())
    whole.wait()

    def strip(c, carry):
        fetch(c, lambda copy: copy.wait())
        cols = pl.ds(pl.multiple_of(c * 256, 256), 256)

        value = dot(amps[...], rows_v[cols, :])
        if not first:
            value = value + total[:, cols]
        if not last:
            out[:, cols] = value
            return carry
        for i in range(6):
            for j in range(2):
                rows = slice(i * BLK, (i + 1) * BLK)
                tile = value[rows, j * BLK:(j + 1) * BLK] * 0.5
                on = ij_ref[i] == ab_ref[2 * c + j]
                where = pl.ds(pl.multiple_of(c * 256 + j * BLK, BLK), BLK)
                out[rows, where] = jnp.where(on, tile, jnp.zeros_like(tile)).astype(BF16)
        return carry

    lax.fori_loop(0, 4, strip, 0)


def product(sym_ij, sym_ab, amps, terms, total=None, last=False):
    depth = amps.shape[1]
    first = total is None
    sizes = [len(block) for _, block in terms]
    n = sum(sizes)

    def kernel(*refs):
        product_kernel(sizes, first, last, *refs)

    scratch = [
        pltpu.VMEM((768, depth), BF16), pltpu.VMEM((1024, depth), BF16), pltpu.SemaphoreType.DMA((5, len(sizes) + 1))
    ]
    return pl.pallas_call(
        kernel,
        out_shape=jax.ShapeDtypeStruct((768, 1024), BF16 if last else F32),
        in_specs=[SMEM] * 2 + [HBM] * (1 + n + (not first)),
        out_specs=VMEM,
        scratch_shapes=scratch + ([] if first else [pltpu.VMEM((768, 1024), F32)]),
        compiler_params=params(60),
        cost_estimate=cost(2 * 768 * 1024 * depth, 8 * 2**20 + 3584 * depth),
    )(sym_ij, sym_ab, amps, *[array for _, block in terms for array in block], *([] if first else [total]))


def body(amp_plus, amp_minus, ints_plus, ints_minus, sym_ij, sym_ab, sym_cd, amp_mask):
    mem = lax.axis_index("mem")
    here = jnp.stack([mem // NZ, mem % NZ]).astype(jnp.int32)

    def go(value, *waits, **way):
        return move(after(value, *waits) if waits else value, **way)

    raw = lax.all_gather(jnp.concatenate([amp_plus, amp_minus], axis=0), "grp", axis=1, tiled=True)

    z0, y0 = ints_plus, ints_minus
    zu, zd, yu, yd = [go(z0, dz=1)], [go(z0, dz=-1)], [go(y0, dy=1)], [go(y0, dy=-1)]
    ones = (zu[0], zd[0], yu[0], yd[0])
    zu.append(go(zu[0], *ones, dz=1))
    zd.append(go(zd[0], *ones, dz=-1))
    y2 = (go(yu[0][:HALF], *ones, dy=1), go(yd[0][HALF:], *ones, dy=-1))
    twos = (zu[1], zd[1]) + y2
    zu.append(go(zu[1], *twos, dz=1))
    zd.append(go(zd[1], *twos, dz=-1))
    c0 = join([(z0,), (zu[0],), (zd[0],), (zu[1],), (zd[1],)])
    c1 = (go(c0, *twos, dy=1), go(c0, *twos, dy=-1))
    w0 = join([(y0,), (yu[0],), (yd[0],), y2])
    threes = (zu[2], zd[2])
    z4 = (go(zu[2][:HALF], *threes, dz=1), go(zd[2][HALF:], *threes, dz=-1))
    d0 = join([(zu[2],), (zd[2],), z4])
    wu, wd = [go(w0, *z4, dz=1)], [go(w0, *z4, dz=-1)]
    c2 = (go(c1[0][:HALF], *c1, dy=1), go(c1[1][HALF:], *c1, dy=-1))
    wu.append(go(wu[0], wd[0], dz=1))
    wd.append(go(wd[0], wu[0], dz=-1))
    d1 = (go(d0, *c2, dy=1), go(d0, *c2, dy=-1))

    def plus(offs, y, block=None):
        return [(0, y, z) for z in offs], block

    def minus(z, block=None):
        return [(1, y, z) for y in (0, -1, 1, 2)], block

    near, far = (0, -1, 1, -2, 2), (-3, 3, 4)
    groups = [
        [plus(near, y) for y in (0, -1, 1, 2)] + [minus(z) for z in (0, -1, 1)],
        [plus(far, y) for y in (0, -1, 1)] + [minus(z) for z in (-2, 2)],
        [plus(far, 2)] + [minus(z) for z in (-3, 3)],
        [minus(4)],
    ]
    amps = mask(here, sym_ij, sym_cd, amp_mask, raw, groups)
    wu.append(go(wu[1], wd[1], amps[0], dz=1))
    wd.append(go(wd[1], wu[1], amps[0], dz=-1))
    blocks = [(c0,), c1[:1], c1[1:], c2, (w0,), (wu[0],), (wd[0],)]
    total = product(sym_ij, sym_ab, amps[0], [(None, block) for block in blocks])
    d2 = (go(d1[0][:HALF], *d1, total, dy=1), go(d1[1][HALF:], *d1, total, dy=-1))
    blocks = [(d0,), d1[:1], d1[1:], (wu[1],), (wd[1],)]
    total = product(sym_ij, sym_ab, amps[1], [(None, block) for block in blocks], total)
    w4 = (go(wu[2][:HALF], wd[2], *d2, dz=1), go(wd[2][HALF:], wu[2], *d2, dz=-1))
    blocks = [d2, (wu[2],), (wd[2],)]
    total = product(sym_ij, sym_ab, amps[2], [(None, block) for block in blocks], total)
    return product(sym_ij, sym_ab, amps[3], [(None, w4)], total, True)


def solution(mesh):
    placed = (
        P("mem", "grp"),
        P("mem", "grp"),
        P("grp", "mem"),
        P("grp", "mem"),
        P("mem"),
        P("grp"),
        P(),
        P("mem", None),
    )
    return jax.shard_map(
        body, mesh=mesh, in_specs=placed, out_specs=P("mem", "grp"), check_vma=False
    )
```

```python
import jax
import jax.numpy as jnp
from jax import lax
from jax.experimental import pallas as pl
from jax.experimental.pallas import tpu as pltpu
from jax.sharding import PartitionSpec as P

BLK = 128
NY, NZ = 4, 8
HALF = 512
BF16 = jnp.bfloat16
F32 = jnp.float32


def perm_of(dy, dz):
    return [
        (8 * y + z, 8 * ((y + dy) % NY) + (z + dz) % NZ) for y in range(NY) for z in range(NZ)
    ]


def move(values, dy=0, dz=0):
    return lax.ppermute(values, "mem", perm_of(dy, dz))


def after(value, *others):
    return lax.optimization_barrier((value,) + others)[0]


SMEM = pl.BlockSpec(memory_space=pltpu.SMEM)
VMEM = pl.BlockSpec(memory_space=pltpu.VMEM)
HBM = pl.BlockSpec(memory_space=pltpu.HBM)


def params(mib):
    return pltpu.CompilerParams(vmem_limit_bytes=mib * 2**20)


def cost(flops, moved):
    return pl.CostEstimate(flops=flops, bytes_accessed=moved, transcendentals=0)


def join_kernel(blocks, *refs):
    out, at, k = refs[-1], 0, 0
    for block in blocks:
        width = block[0].shape[1]
        if len(block) == 1:
            out[:, at:at + width] = refs[k][...]
        else:
            out[:HALF, at:at + width] = refs[k][...]
            out[HALF:, at:at + width] = refs[k + 1][...]
        at += width
        k += len(block)


def join(blocks):
    arrays = [array for block in blocks for array in block]
    full = sum(block[0].shape[1] for block in blocks)

    def kernel(*refs):
        join_kernel(blocks, *refs)

    return pl.pallas_call(
        kernel,
        out_shape=jax.ShapeDtypeStruct((2 * HALF, full), BF16),
        in_specs=[VMEM] * len(arrays),
        out_specs=VMEM,
        compiler_params=params(8),
        cost_estimate=cost(0, 8 * HALF * full),
    )(*arrays)


def dot(left, right):
    return lax.dot_general(left, right, (((1,), (1,)), ((), ())), preferred_element_type=F32)


def tiles_of(terms):
    return [tile for tiles, _ in terms for tile in tiles]


def mask_kernel(parts, here_ref, ij_ref, cd_ref, mask_ref, raw_hbm, *refs):
    outs, raw, laid, sem = refs[:len(parts)], refs[-2 - len(parts)], refs[-1 - len(parts):-1], refs[-1]
    fetch = pltpu.make_async_copy(raw_hbm, raw, sem.at[len(parts)])
    fetch.start()
    y, z = here_ref[0], here_ref[1]
    fetch.wait()
    copies = []
    for p, (target, tiles) in enumerate(zip(laid, parts)):
        for k, (panel, off_y, off_z) in enumerate(tiles):
            tile = 8 * ((y + off_y) & (NY - 1)) + ((z + off_z) & (NZ - 1))
            cols = pl.ds(pl.multiple_of(tile * BLK, BLK), BLK)
            label = cd_ref[tile]
            for row in range(6):
                on = (ij_ref[row] == label) & (mask_ref[row, tile] == 1)
                kept = raw[pl.ds(panel * 768 + row * BLK, BLK), cols]
                target[row * BLK:(row + 1) * BLK, k * BLK:(k + 1) * BLK] = jnp.where(on, kept, jnp.zeros_like(kept))
        copies.append(pltpu.make_async_copy(target, outs[p], sem.at[p]))
        copies[-1].start()
    for copy in copies:
        copy.wait()


def mask(here, sym_ij, sym_cd, amp_mask, raw, groups):
    parts = [tiles_of(terms) for terms in groups]
    shapes = [(768, len(tiles) * BLK) for tiles in parts]

    def kernel(*refs):
        mask_kernel(parts, *refs)

    return pl.pallas_call(
        kernel,
        out_shape=[jax.ShapeDtypeStruct(shape, BF16) for shape in shapes],
        in_specs=[SMEM] * 4 + [HBM],
        out_specs=[HBM] * len(shapes),
        scratch_shapes=[pltpu.VMEM((1536, 4096), BF16)]
        + [pltpu.VMEM(shape, BF16) for shape in shapes]
        + [pltpu.SemaphoreType.DMA((len(shapes) + 1,))],
        compiler_params=params(60),
        cost_estimate=cost(0, 25 * 2**20),
    )(here, sym_ij, sym_cd, amp_mask, raw)


def product_kernel(sizes, first, last, ij_ref, ab_ref, amps_hbm, *refs):
    n = sum(sizes)
    ints, refs = refs[:n], refs[n:]
    if first:
        out, amps, rows_v, sem = refs
    else:
        total_hbm, out, amps, rows_v, sem, total = refs

    def fetch(c, act):
        rows = pl.ds(pl.multiple_of(c * 256, 256), 256)
        at, k = 0, 0
        for b, size in enumerate(sizes):
            width = ints[k].shape[1]
            to = rows_v.at[rows, pl.ds(at, width)]
            if size == 1:
                act(pltpu.make_async_copy(ints[k].at[rows, :], to, sem.at[c, b]))
            else:
                part = pl.ds(pl.multiple_of((c & 1) * 256, 256), 256)

                @pl.when(c < 2)
                def _():
                    act(pltpu.make_async_copy(ints[k].at[part, :], to, sem.at[c, b]))

                @pl.when(c >= 2)
                def _():
                    act(pltpu.make_async_copy(ints[k + 1].at[part, :], to, sem.at[c, b]))
            at += width
            k += size
        if not first:
            act(pltpu.make_async_copy(total_hbm.at[:, rows], total.at[:, rows], sem.at[c, len(sizes)]))

    whole = pltpu.make_async_copy(amps_hbm, amps, sem.at[4, 0])
    whole.start()
    for c in range(4):
        fetch(jnp.int32(c), lambda copy: copy.start())
    whole.wait()

    def strip(c, carry):
        fetch(c, lambda copy: copy.wait())
        cols = pl.ds(pl.multiple_of(c * 256, 256), 256)

        value = dot(amps[...], rows_v[cols, :])
        if not first:
            value = value + total[:, cols]
        if not last:
            out[:, cols] = value
            return carry
        for i in range(6):
            for j in range(2):
                rows = slice(i * BLK, (i + 1) * BLK)
                tile = value[rows, j * BLK:(j + 1) * BLK] * 0.5
                on = ij_ref[i] == ab_ref[2 * c + j]
                where = pl.ds(pl.multiple_of(c * 256 + j * BLK, BLK), BLK)
                out[rows, where] = jnp.where(on, tile, jnp.zeros_like(tile)).astype(BF16)
        return carry

    lax.fori_loop(0, 4, strip, 0)


def product(sym_ij, sym_ab, amps, terms, total=None, last=False):
    depth = amps.shape[1]
    first = total is None
    sizes = [len(block) for _, block in terms]
    n = sum(sizes)

    def kernel(*refs):
        product_kernel(sizes, first, last, *refs)

    scratch = [
        pltpu.VMEM((768, depth), BF16), pltpu.VMEM((1024, depth), BF16), pltpu.SemaphoreType.DMA((5, len(sizes) + 1))
    ]
    return pl.pallas_call(
        kernel,
        out_shape=jax.ShapeDtypeStruct((768, 1024), BF16 if last else F32),
        in_specs=[SMEM] * 2 + [HBM] * (1 + n + (not first)),
        out_specs=VMEM,
        scratch_shapes=scratch + ([] if first else [pltpu.VMEM((768, 1024), F32)]),
        compiler_params=params(60),
        cost_estimate=cost(2 * 768 * 1024 * depth, 8 * 2**20 + 3584 * depth),
    )(sym_ij, sym_ab, amps, *[array for _, block in terms for array in block], *([] if first else [total]))


def body(amp_plus, amp_minus, ints_plus, ints_minus, sym_ij, sym_ab, sym_cd, amp_mask):
    mem = lax.axis_index("mem")
    here = jnp.stack([mem // NZ, mem % NZ]).astype(jnp.int32)

    def go(value, *waits, **way):
        return move(after(value, *waits) if waits else value, **way)

    raw = lax.all_gather(jnp.concatenate([amp_plus, amp_minus], axis=0), "grp", axis=1, tiled=True)

    z0, y0 = ints_plus, ints_minus
    zu, zd, yu, yd = [go(z0, dz=1)], [go(z0, dz=-1)], [go(y0, dy=1)], [go(y0, dy=-1)]
    ones = (zu[0], zd[0], yu[0])
    zu.append(go(zu[0], *ones, dz=1))
    zd.append(go(zd[0], *ones, dz=-1))
    y2 = (go(yu[0], *ones, yd[0], dy=1),)
    twos = (zu[1], zd[1])
    zu.append(go(zu[1], *twos, dz=1))
    zd.append(go(zd[1], *twos, dz=-1))
    c0 = join([(z0,), (zu[0],), (zd[0],), (zu[1],), (zd[1],)])
    c1 = (go(c0, *y2, dy=1), go(c0, *y2, dy=-1))
    w0 = join([(y0,), (yu[0],), (yd[0],), y2])
    threes = (zu[2], zd[2])
    wu, wd = [go(w0, *threes, dz=1)], [go(w0, *threes, dz=-1)]
    z4 = (go(zu[2], dz=1),)
    d0 = join([(zu[2],), (zd[2],), z4])
    c2 = (go(c1[0][:HALF], *c1, dy=1), go(c1[1][HALF:], *c1, dy=-1))
    wu.append(go(wu[0], wd[0], *z4, dz=1))
    wd.append(go(wd[0], wu[0], *z4, dz=-1))
    d1 = (go(d0, *c2, dy=1), go(d0, *c2, dy=-1))

    def plus(offs, y, block=None):
        return [(0, y, z) for z in offs], block

    def minus(z, block=None):
        return [(1, y, z) for y in (0, -1, 1, 2)], block

    near, far = (0, -1, 1, -2, 2), (-3, 3, 4)
    groups = [
        [plus(near, y) for y in (0, -1, 1)],
        [plus(near, 2)] + [plus(far, y) for y in (0, -1, 1)] + [minus(z) for z in (0, -1, 1, -2, 2)],
        [plus(far, 2)] + [minus(z) for z in (-3, 3)],
        [minus(4)],
    ]
    amps = mask(here, sym_ij, sym_cd, amp_mask, raw, groups)
    wu.append(go(wu[1], wd[1], amps[0], dz=1))
    wd.append(go(wd[1], wu[1], amps[0], dz=-1))
    blocks = [(c0,), c1[:1], c1[1:]]
    total = product(sym_ij, sym_ab, amps[0], [(None, block) for block in blocks])
    d2 = (go(d1[0][:HALF], *d1, total, dy=1), go(d1[1][HALF:], *d1, total, dy=-1))
    blocks = [c2, (d0,), d1[:1], d1[1:], (w0,), (wu[0],), (wd[0],), (wu[1],), (wd[1],)]
    total = product(sym_ij, sym_ab, amps[1], [(None, block) for block in blocks], total)
    w4 = (go(wu[2][:HALF], wd[2], *d2, total, dz=1), go(wd[2][HALF:], wu[2], *d2, total, dz=-1))
    blocks = [d2, (wu[2],), (wd[2],)]
    total = product(sym_ij, sym_ab, amps[2], [(None, block) for block in blocks], total)
    return product(sym_ij, sym_ab, amps[3], [(None, w4)], total, True)


def solution(mesh):
    placed = (
        P("mem", "grp"),
        P("mem", "grp"),
        P("grp", "mem"),
        P("grp", "mem"),
        P("mem"),
        P("grp"),
        P(),
        P("mem", None),
    )
    return jax.shard_map(
        body, mesh=mesh, in_specs=placed, out_specs=P("mem", "grp"), check_vma=False
    )
```

```python
import jax
import jax.numpy as jnp
from jax import lax
from jax.experimental import pallas as pl
from jax.experimental.pallas import tpu as pltpu
from jax.sharding import PartitionSpec as P

BLK = 128
NY, NZ = 4, 8
HALF = 512
BF16 = jnp.bfloat16
F32 = jnp.float32


def perm_of(dy, dz):
    return [
        (8 * y + z, 8 * ((y + dy) % NY) + (z + dz) % NZ) for y in range(NY) for z in range(NZ)
    ]


def move(values, dy=0, dz=0):
    return lax.ppermute(values, "mem", perm_of(dy, dz))


def after(value, *others):
    return lax.optimization_barrier((value,) + others)[0]


SMEM = pl.BlockSpec(memory_space=pltpu.SMEM)
VMEM = pl.BlockSpec(memory_space=pltpu.VMEM)
HBM = pl.BlockSpec(memory_space=pltpu.HBM)


def params(mib):
    return pltpu.CompilerParams(vmem_limit_bytes=mib * 2**20)


def cost(flops, moved):
    return pl.CostEstimate(flops=flops, bytes_accessed=moved, transcendentals=0)


def join_kernel(blocks, *refs):
    out, at, k = refs[-1], 0, 0
    for block in blocks:
        width = block[0].shape[1]
        if len(block) == 1:
            out[:, at:at + width] = refs[k][...]
        else:
            out[:HALF, at:at + width] = refs[k][...]
            out[HALF:, at:at + width] = refs[k + 1][...]
        at += width
        k += len(block)


def join(blocks):
    arrays = [array for block in blocks for array in block]
    full = sum(block[0].shape[1] for block in blocks)

    def kernel(*refs):
        join_kernel(blocks, *refs)

    return pl.pallas_call(
        kernel,
        out_shape=jax.ShapeDtypeStruct((2 * HALF, full), BF16),
        in_specs=[VMEM] * len(arrays),
        out_specs=VMEM,
        compiler_params=params(8),
        cost_estimate=cost(0, 8 * HALF * full),
    )(*arrays)


def dot(left, right):
    return lax.dot_general(left, right, (((1,), (1,)), ((), ())), preferred_element_type=F32)


def mask_kernel(parts, here_ref, ij_ref, cd_ref, mask_ref, raw_hbm, *refs):
    outs, raw, laid, sem = refs[:len(parts)], refs[-2 - len(parts)], refs[-1 - len(parts):-1], refs[-1]
    fetch = pltpu.make_async_copy(raw_hbm, raw, sem.at[len(parts)])
    fetch.start()
    y, z = here_ref[0], here_ref[1]
    fetch.wait()
    copies = []
    for p, (target, tiles) in enumerate(zip(laid, parts)):
        for k, (off_y, off_z) in enumerate(tiles):
            tile = 8 * ((y + off_y) & (NY - 1)) + ((z + off_z) & (NZ - 1))
            cols = pl.ds(pl.multiple_of(tile * BLK, BLK), BLK)
            label = cd_ref[tile]
            for row in range(6):
                on = (ij_ref[row] == label) & (mask_ref[row, tile] == 1)
                kept = raw[row * BLK:(row + 1) * BLK, cols]
                target[row * BLK:(row + 1) * BLK, k * BLK:(k + 1) * BLK] = jnp.where(on, kept, jnp.zeros_like(kept))
        copies.append(pltpu.make_async_copy(target, outs[p], sem.at[p]))
        copies[-1].start()
    for copy in copies:
        copy.wait()


def mask(here, sym_ij, sym_cd, amp_mask, raw, *parts):
    shapes = [(768, len(tiles) * BLK) for tiles in parts]

    def kernel(*refs):
        mask_kernel(parts, *refs)

    return pl.pallas_call(
        kernel,
        out_shape=[jax.ShapeDtypeStruct(shape, BF16) for shape in shapes],
        in_specs=[SMEM] * 4 + [HBM],
        out_specs=[HBM] * len(shapes),
        scratch_shapes=[pltpu.VMEM((768, 4096), BF16)]
        + [pltpu.VMEM(shape, BF16) for shape in shapes]
        + [pltpu.SemaphoreType.DMA((len(shapes) + 1,))],
        compiler_params=params(60),
        cost_estimate=cost(0, 12 * 2**20),
    )(here, sym_ij, sym_cd, amp_mask, raw)


def product_kernel(sizes, first, last, ij_ref, ab_ref, amps_hbm, *refs):
    n = sum(sizes)
    ints, refs = refs[:n], refs[n:]
    if first:
        out, amps, rows_v, sem = refs
    else:
        total_hbm, out, amps, rows_v, sem, total = refs

    def fetch(c, act):
        rows = pl.ds(pl.multiple_of(c * 256, 256), 256)
        at, k = 0, 0
        for b, size in enumerate(sizes):
            width = ints[k].shape[1]
            to = rows_v.at[rows, pl.ds(at, width)]
            if size == 1:
                act(pltpu.make_async_copy(ints[k].at[rows, :], to, sem.at[c, b]))
            else:
                part = pl.ds(pl.multiple_of((c & 1) * 256, 256), 256)

                @pl.when(c < 2)
                def _():
                    act(pltpu.make_async_copy(ints[k].at[part, :], to, sem.at[c, b]))

                @pl.when(c >= 2)
                def _():
                    act(pltpu.make_async_copy(ints[k + 1].at[part, :], to, sem.at[c, b]))
            at += width
            k += size
        if not first:
            act(pltpu.make_async_copy(total_hbm.at[:, rows], total.at[:, rows], sem.at[c, len(sizes)]))

    whole = pltpu.make_async_copy(amps_hbm, amps, sem.at[4, 0])
    whole.start()
    for c in range(4):
        fetch(jnp.int32(c), lambda copy: copy.start())
    whole.wait()

    def strip(c, carry):
        fetch(c, lambda copy: copy.wait())
        cols = pl.ds(pl.multiple_of(c * 256, 256), 256)

        value = dot(amps[...], rows_v[cols, :])
        if not first:
            value = value + total[:, cols]
        if not last:
            out[:, cols] = value
            return carry
        for i in range(6):
            for j in range(2):
                rows = slice(i * BLK, (i + 1) * BLK)
                tile = value[rows, j * BLK:(j + 1) * BLK] * 0.5
                on = ij_ref[i] == ab_ref[2 * c + j]
                where = pl.ds(pl.multiple_of(c * 256 + j * BLK, BLK), BLK)
                out[rows, where] = jnp.where(on, tile, jnp.zeros_like(tile)).astype(BF16)
        return carry

    lax.fori_loop(0, 4, strip, 0)


def product(sym_ij, sym_ab, amps, blocks, total=None, last=False):
    depth = amps.shape[1]
    first = total is None
    sizes = [len(block) for block in blocks]
    n = sum(sizes)

    def kernel(*refs):
        product_kernel(sizes, first, last, *refs)

    scratch = [
        pltpu.VMEM((768, depth), BF16), pltpu.VMEM((1024, depth), BF16), pltpu.SemaphoreType.DMA((5, len(sizes) + 1))
    ]
    return pl.pallas_call(
        kernel,
        out_shape=jax.ShapeDtypeStruct((768, 1024), BF16 if last else F32),
        in_specs=[SMEM] * 2 + [HBM] * (1 + n + (not first)),
        out_specs=VMEM,
        scratch_shapes=scratch + ([] if first else [pltpu.VMEM((768, 1024), F32)]),
        compiler_params=params(60),
        cost_estimate=cost(2 * 768 * 1024 * depth, 8 * 2**20 + 3584 * depth),
    )(sym_ij, sym_ab, amps, *[array for block in blocks for array in block], *([] if first else [total]))


def body(amp_plus, amp_minus, ints_plus, ints_minus, sym_ij, sym_ab, sym_cd, amp_mask):
    mem = lax.axis_index("mem")
    here = jnp.stack([mem // NZ, mem % NZ]).astype(jnp.int32)

    def go(value, *waits, **way):
        return move(after(value, *waits) if waits else value, **way)

    raw_plus = lax.all_gather(amp_plus, "grp", axis=1, tiled=True)
    raw_minus = lax.all_gather(amp_minus, "grp", axis=1, tiled=True)

    z0, y0 = ints_plus, ints_minus
    zu, zd, yu, yd = [go(z0, dz=1)], [go(z0, dz=-1)], [go(y0, dy=1)], [go(y0, dy=-1)]
    ones = (zu[0], zd[0], yu[0])
    zu.append(go(zu[0], *ones, dz=1))
    zd.append(go(zd[0], *ones, dz=-1))
    y2 = (go(yu[0], *ones, yd[0], dy=1),)
    twos = (zu[1], zd[1])
    zu.append(go(zu[1], *twos, dz=1))
    zd.append(go(zd[1], *twos, dz=-1))
    c0 = join([(z0,), (zu[0],), (zd[0],), (zu[1],), (zd[1],)])
    c1 = (go(c0, *y2, dy=1), go(c0, *y2, dy=-1))
    w0 = join([(y0,), (yu[0],), (yd[0],), y2])
    threes = (zu[2], zd[2])
    wu, wd = [go(w0, *threes, dz=1)], [go(w0, *threes, dz=-1)]
    z4 = (go(zu[2], dz=1),)
    d0 = join([(zu[2],), (zd[2],), z4])
    c2 = (go(c1[0][:HALF], *c1, dy=1), go(c1[1][HALF:], *c1, dy=-1))
    wu.append(go(wu[0], wd[0], *z4, *c1, dz=1))
    wd.append(go(wd[0], wu[0], *z4, *c1, dz=-1))

    def plus(offs, *ys):
        return [(y, z) for y in ys for z in offs]

    def minus(*zs):
        return [(y, z) for z in zs for y in (0, -1, 1, 2)]

    def add(amps, blocks, *rest):
        return product(sym_ij, sym_ab, amps, blocks, *rest)

    labels = (here, sym_ij, sym_cd, amp_mask)
    near, far = (0, -1, 1, -2, 2), (-3, 3, 4)
    tp = mask(*labels, raw_plus, plus(near, 0, -1, 1), plus(near, 2) + plus(far, 0), plus(far, -1, 1, 2))
    total = add(tp[0], [(c0,), c1[:1], c1[1:]])
    d1 = (go(d0, *c2, total, dy=1), go(d0, *c2, total, dy=-1))
    total = add(tp[1], [c2, (d0,)], total)
    wu.append(go(wu[1], wd[1], total, dz=1))
    wd.append(go(wd[1], wu[1], total, dz=-1))
    tm = mask(*labels, raw_minus, minus(0, -1, 1, -2, 2), minus(-3, 3), minus(4))
    d2 = (go(d1[0][:HALF], *d1, tm[0], dy=1), go(d1[1][HALF:], *d1, tm[0], dy=-1))
    total = add(tm[0], [(w0,), (wu[0],), (wd[0],), (wu[1],), (wd[1],)], total)
    w4 = (go(wu[2][:HALF], wd[2], *d2, total, dz=1), go(wd[2][HALF:], wu[2], *d2, total, dz=-1))
    total = add(tp[2], [d1[:1], d1[1:], d2], total)
    total = add(tm[1], [(wu[2],), (wd[2],)], total)
    return add(tm[2], [w4], total, True)


def solution(mesh):
    placed = (
        P("mem", "grp"),
        P("mem", "grp"),
        P("grp", "mem"),
        P("grp", "mem"),
        P("mem"),
        P("grp"),
        P(),
        P("mem", None),
    )
    return jax.shard_map(
        body, mesh=mesh, in_specs=placed, out_specs=P("mem", "grp"), check_vma=False
    )
```

```python
import jax
import jax.numpy as jnp
from jax import lax
from jax.experimental import pallas as pl
from jax.experimental.pallas import tpu as pltpu
from jax.sharding import PartitionSpec as P

BLK = 128
NY, NZ = 4, 8
HALF = 512
BF16 = jnp.bfloat16
F32 = jnp.float32


def perm_of(dy, dz):
    return [
        (8 * y + z, 8 * ((y + dy) % NY) + (z + dz) % NZ) for y in range(NY) for z in range(NZ)
    ]


def move(values, dy=0, dz=0):
    return lax.ppermute(values, "mem", perm_of(dy, dz))


def after(value, *others):
    return lax.optimization_barrier((value,) + others)[0]


SMEM = pl.BlockSpec(memory_space=pltpu.SMEM)
VMEM = pl.BlockSpec(memory_space=pltpu.VMEM)
HBM = pl.BlockSpec(memory_space=pltpu.HBM)


def params(mib):
    return pltpu.CompilerParams(vmem_limit_bytes=mib * 2**20)


def cost(flops, moved):
    return pl.CostEstimate(flops=flops, bytes_accessed=moved, transcendentals=0)


def join_kernel(blocks, *refs):
    out, at, k = refs[-1], 0, 0
    for block in blocks:
        width = block[0].shape[1]
        if len(block) == 1:
            out[:, at:at + width] = refs[k][...]
        else:
            out[:HALF, at:at + width] = refs[k][...]
            out[HALF:, at:at + width] = refs[k + 1][...]
        at += width
        k += len(block)


def join(blocks):
    arrays = [array for block in blocks for array in block]
    full = sum(block[0].shape[1] for block in blocks)

    def kernel(*refs):
        join_kernel(blocks, *refs)

    return pl.pallas_call(
        kernel,
        out_shape=jax.ShapeDtypeStruct((2 * HALF, full), BF16),
        in_specs=[VMEM] * len(arrays),
        out_specs=VMEM,
        compiler_params=params(8),
        cost_estimate=cost(0, 8 * HALF * full),
    )(*arrays)


def dot(left, right):
    return lax.dot_general(left, right, (((1,), (1,)), ((), ())), preferred_element_type=F32)


def mask_kernel(parts, here_ref, ij_ref, cd_ref, mask_ref, raw_hbm, *refs):
    outs, raw, laid, sem = refs[:len(parts)], refs[-2 - len(parts)], refs[-1 - len(parts):-1], refs[-1]
    fetch = pltpu.make_async_copy(raw_hbm, raw, sem.at[len(parts)])
    fetch.start()
    y, z = here_ref[0], here_ref[1]
    fetch.wait()
    copies = []
    for p, (target, tiles) in enumerate(zip(laid, parts)):
        for k, (off_y, off_z) in enumerate(tiles):
            tile = 8 * ((y + off_y) & (NY - 1)) + ((z + off_z) & (NZ - 1))
            cols = pl.ds(pl.multiple_of(tile * BLK, BLK), BLK)
            label = cd_ref[tile]
            for row in range(6):
                on = (ij_ref[row] == label) & (mask_ref[row, tile] == 1)
                kept = raw[row * BLK:(row + 1) * BLK, cols]
                target[row * BLK:(row + 1) * BLK, k * BLK:(k + 1) * BLK] = jnp.where(on, kept, jnp.zeros_like(kept))
        copies.append(pltpu.make_async_copy(target, outs[p], sem.at[p]))
        copies[-1].start()
    for copy in copies:
        copy.wait()


def mask(here, sym_ij, sym_cd, amp_mask, raw, *parts):
    shapes = [(768, len(tiles) * BLK) for tiles in parts]

    def kernel(*refs):
        mask_kernel(parts, *refs)

    return pl.pallas_call(
        kernel,
        out_shape=[jax.ShapeDtypeStruct(shape, BF16) for shape in shapes],
        in_specs=[SMEM] * 4 + [HBM],
        out_specs=[HBM] * len(shapes),
        scratch_shapes=[pltpu.VMEM((768, 4096), BF16)]
        + [pltpu.VMEM(shape, BF16) for shape in shapes]
        + [pltpu.SemaphoreType.DMA((len(shapes) + 1,))],
        compiler_params=params(60),
        cost_estimate=cost(0, 12 * 2**20),
    )(here, sym_ij, sym_cd, amp_mask, raw)


def product_kernel(pieces, sizes, first, last, ij_ref, ab_ref, *refs):
    n = sum(sizes)
    amps_hbm, ints, refs = refs[:pieces], refs[pieces:pieces + n], refs[pieces + n:]
    if first:
        out, amps, rows_v, sem = refs
    else:
        total_hbm, out, amps, rows_v, sem, total = refs

    def fetch(c, act):
        rows = pl.ds(pl.multiple_of(c * 256, 256), 256)
        at, k = 0, 0
        for b, size in enumerate(sizes):
            width = ints[k].shape[1]
            to = rows_v.at[rows, pl.ds(at, width)]
            if size == 1:
                act(pltpu.make_async_copy(ints[k].at[rows, :], to, sem.at[c, b]))
            else:
                part = pl.ds(pl.multiple_of((c & 1) * 256, 256), 256)

                @pl.when(c < 2)
                def _():
                    act(pltpu.make_async_copy(ints[k].at[part, :], to, sem.at[c, b]))

                @pl.when(c >= 2)
                def _():
                    act(pltpu.make_async_copy(ints[k + 1].at[part, :], to, sem.at[c, b]))
            at += width
            k += size
        if not first:
            act(pltpu.make_async_copy(total_hbm.at[:, rows], total.at[:, rows], sem.at[c, len(sizes)]))

    whole, at = [], 0
    for k, piece in enumerate(amps_hbm):
        width = piece.shape[1]
        whole.append(pltpu.make_async_copy(piece, amps.at[:, pl.ds(at, width)], sem.at[4, k]))
        whole[-1].start()
        at += width
    for c in range(4):
        fetch(jnp.int32(c), lambda copy: copy.start())
    for copy in whole:
        copy.wait()

    def strip(c, carry):
        fetch(c, lambda copy: copy.wait())
        cols = pl.ds(pl.multiple_of(c * 256, 256), 256)

        value = dot(amps[...], rows_v[cols, :])
        if not first:
            value = value + total[:, cols]
        if not last:
            out[:, cols] = value
            return carry
        for i in range(6):
            for j in range(2):
                rows = slice(i * BLK, (i + 1) * BLK)
                tile = value[rows, j * BLK:(j + 1) * BLK] * 0.5
                on = ij_ref[i] == ab_ref[2 * c + j]
                where = pl.ds(pl.multiple_of(c * 256 + j * BLK, BLK), BLK)
                out[rows, where] = jnp.where(on, tile, jnp.zeros_like(tile)).astype(BF16)
        return carry

    lax.fori_loop(0, 4, strip, 0)


def product(sym_ij, sym_ab, amps, blocks, total=None, last=False):
    depth = sum(piece.shape[1] for piece in amps)
    first = total is None
    sizes = [len(block) for block in blocks]
    n = sum(sizes)

    def kernel(*refs):
        product_kernel(len(amps), sizes, first, last, *refs)

    scratch = [
        pltpu.VMEM((768, depth), BF16), pltpu.VMEM((1024, depth), BF16), pltpu.SemaphoreType.DMA((5, len(sizes) + 1))
    ]
    return pl.pallas_call(
        kernel,
        out_shape=jax.ShapeDtypeStruct((768, 1024), BF16 if last else F32),
        in_specs=[SMEM] * 2 + [HBM] * (len(amps) + n + (not first)),
        out_specs=VMEM,
        scratch_shapes=scratch + ([] if first else [pltpu.VMEM((768, 1024), F32)]),
        compiler_params=params(60),
        cost_estimate=cost(2 * 768 * 1024 * depth, 8 * 2**20 + 3584 * depth),
    )(sym_ij, sym_ab, *amps, *[array for block in blocks for array in block], *([] if first else [total]))


def body(amp_plus, amp_minus, ints_plus, ints_minus, sym_ij, sym_ab, sym_cd, amp_mask):
    mem = lax.axis_index("mem")
    here = jnp.stack([mem // NZ, mem % NZ]).astype(jnp.int32)

    def go(value, *waits, **way):
        return move(after(value, *waits) if waits else value, **way)

    raw_plus = lax.all_gather(amp_plus, "grp", axis=1, tiled=True)
    raw_minus = lax.all_gather(amp_minus, "grp", axis=1, tiled=True)

    z0, y0 = ints_plus, ints_minus
    zu, zd, yu, yd = [go(z0, dz=1)], [go(z0, dz=-1)], [go(y0, dy=1)], [go(y0, dy=-1)]
    ones = (zu[0], zd[0], yu[0])
    zu.append(go(zu[0], *ones, dz=1))
    zd.append(go(zd[0], *ones, dz=-1))
    y2 = (go(yu[0], *ones, yd[0], dy=1),)
    twos = (zu[1], zd[1])
    zu.append(go(zu[1], *twos, dz=1))
    zd.append(go(zd[1], *twos, dz=-1))
    c0 = join([(z0,), (zu[0],), (zd[0],), (zu[1],), (zd[1],)])
    c1 = (go(c0, *y2, dy=1), go(c0, *y2, dy=-1))
    w0 = join([(y0,), (yu[0],), (yd[0],), y2])
    threes = (zu[2], zd[2])
    wu, wd = [go(w0, *threes, dz=1)], [go(w0, *threes, dz=-1)]

    def plus(offs, *ys):
        return [(y, z) for y in ys for z in offs]

    def minus(*zs):
        return [(y, z) for z in zs for y in (0, -1, 1, 2)]

    def add(amps, blocks, *rest):
        return product(sym_ij, sym_ab, amps, blocks, *rest)

    labels = (here, sym_ij, sym_cd, amp_mask)
    near, far = (0, -1, 1, -2, 2), (-3, 3, 4)
    tp = mask(*labels, raw_plus, plus(near, 0, -1, 1) + plus(far, 0), plus(far, -1, 1), plus(near, 2) + plus(far, 2))
    z4 = (go(zu[2], tp[0], dz=1),)
    d0 = join([(zu[2],), (zd[2],), z4])
    c2 = (go(c1[0][:HALF], *c1, tp[0], dy=1), go(c1[1][HALF:], *c1, tp[0], dy=-1))
    wu.append(go(wu[0], wd[0], *z4, *c1, dz=1))
    wd.append(go(wd[0], wu[0], *z4, *c1, dz=-1))
    total = add(tp[:1], [(c0,), c1[:1], c1[1:], (d0,)])
    d1 = (go(d0, *c2, total, dy=1), go(d0, *c2, total, dy=-1))
    wu.append(go(wu[1], wd[1], dz=1))
    wd.append(go(wd[1], wu[1], dz=-1))
    tm = mask(*labels, raw_minus, minus(0, -1, 1, -2, 2), minus(-3, 3), minus(4))
    d2 = (go(d1[0][:HALF], *d1, tm[0], dy=1), go(d1[1][HALF:], *d1, tm[0], dy=-1))
    total = add(
        [tm[0], tp[1]], [(w0,), (wu[0],), (wd[0],), (wu[1],), (wd[1],), d1[:1], d1[1:]], total
    )
    w4 = (go(wu[2][:HALF], wd[2], *d2, total, dz=1), go(wd[2][HALF:], wu[2], *d2, total, dz=-1))
    total = add([tp[2], tm[1]], [c2, d2, (wu[2],), (wd[2],)], total)
    return add(tm[2:], [w4], total, True)


def solution(mesh):
    placed = (
        P("mem", "grp"),
        P("mem", "grp"),
        P("grp", "mem"),
        P("grp", "mem"),
        P("mem"),
        P("grp"),
        P(),
        P("mem", None),
    )
    return jax.shard_map(
        body, mesh=mesh, in_specs=placed, out_specs=P("mem", "grp"), check_vma=False
    )
```

```python
import jax
import jax.numpy as jnp
from jax import lax
from jax.experimental import pallas as pl
from jax.experimental.pallas import tpu as pltpu
from jax.sharding import PartitionSpec as P

BLK = 128
NY, NZ = 4, 8
HALF = 512
BF16 = jnp.bfloat16
F32 = jnp.float32


def perm_of(dy, dz):
    return [
        (8 * y + z, 8 * ((y + dy) % NY) + (z + dz) % NZ) for y in range(NY) for z in range(NZ)
    ]


def move(values, dy=0, dz=0):
    return lax.ppermute(values, "mem", perm_of(dy, dz))


def after(value, *others):
    return lax.optimization_barrier((value,) + others)[0]


SMEM = pl.BlockSpec(memory_space=pltpu.SMEM)
VMEM = pl.BlockSpec(memory_space=pltpu.VMEM)
HBM = pl.BlockSpec(memory_space=pltpu.HBM)


def params(mib):
    return pltpu.CompilerParams(vmem_limit_bytes=mib * 2**20)


def cost(flops, moved):
    return pl.CostEstimate(flops=flops, bytes_accessed=moved, transcendentals=0)


def join_kernel(blocks, *refs):
    out, at, k = refs[-1], 0, 0
    for block in blocks:
        width = block[0].shape[1]
        if len(block) == 1:
            out[:, at:at + width] = refs[k][...]
        else:
            out[:HALF, at:at + width] = refs[k][...]
            out[HALF:, at:at + width] = refs[k + 1][...]
        at += width
        k += len(block)


def join(blocks):
    arrays = [array for block in blocks for array in block]
    full = sum(block[0].shape[1] for block in blocks)

    def kernel(*refs):
        join_kernel(blocks, *refs)

    return pl.pallas_call(
        kernel,
        out_shape=jax.ShapeDtypeStruct((2 * HALF, full), BF16),
        in_specs=[VMEM] * len(arrays),
        out_specs=VMEM,
        compiler_params=params(8),
        cost_estimate=cost(0, 8 * HALF * full),
    )(*arrays)


def dot(left, right):
    return lax.dot_general(left, right, (((1,), (1,)), ((), ())), preferred_element_type=F32)


def mask_kernel(parts, here_ref, ij_ref, cd_ref, mask_ref, raw_hbm, *refs):
    outs, raw, laid, sem = refs[:len(parts)], refs[-2 - len(parts)], refs[-1 - len(parts):-1], refs[-1]
    fetch = pltpu.make_async_copy(raw_hbm, raw, sem.at[len(parts)])
    fetch.start()
    y, z = here_ref[0], here_ref[1]
    fetch.wait()
    copies = []
    for p, (target, tiles) in enumerate(zip(laid, parts)):
        for k, (off_y, off_z) in enumerate(tiles):
            tile = 8 * ((y + off_y) & (NY - 1)) + ((z + off_z) & (NZ - 1))
            cols = pl.ds(pl.multiple_of(tile * BLK, BLK), BLK)
            label = cd_ref[tile]
            for row in range(6):
                on = (ij_ref[row] == label) & (mask_ref[row, tile] == 1)
                kept = raw[row * BLK:(row + 1) * BLK, cols]
                target[row * BLK:(row + 1) * BLK, k * BLK:(k + 1) * BLK] = jnp.where(on, kept, jnp.zeros_like(kept))
        copies.append(pltpu.make_async_copy(target, outs[p], sem.at[p]))
        copies[-1].start()
    for copy in copies:
        copy.wait()


def mask(here, sym_ij, sym_cd, amp_mask, raw, *parts):
    shapes = [(768, len(tiles) * BLK) for tiles in parts]

    def kernel(*refs):
        mask_kernel(parts, *refs)

    return pl.pallas_call(
        kernel,
        out_shape=[jax.ShapeDtypeStruct(shape, BF16) for shape in shapes],
        in_specs=[SMEM] * 4 + [HBM],
        out_specs=[HBM] * len(shapes),
        scratch_shapes=[pltpu.VMEM((768, 4096), BF16)]
        + [pltpu.VMEM(shape, BF16) for shape in shapes]
        + [pltpu.SemaphoreType.DMA((len(shapes) + 1,))],
        compiler_params=params(60),
        cost_estimate=cost(0, 12 * 2**20),
    )(here, sym_ij, sym_cd, amp_mask, raw)


def product_kernel(pieces, sizes, first, last, ij_ref, ab_ref, *refs):
    n = sum(sizes)
    amps_hbm, ints, refs = refs[:pieces], refs[pieces:pieces + n], refs[pieces + n:]
    if first:
        out, amps, rows_v, sem = refs
    else:
        total_hbm, out, amps, rows_v, sem, total = refs

    def fetch(c, act):
        rows = pl.ds(pl.multiple_of(c * 256, 256), 256)
        at, k = 0, 0
        for b, size in enumerate(sizes):
            width = ints[k].shape[1]
            to = rows_v.at[rows, pl.ds(at, width)]
            if size == 1:
                act(pltpu.make_async_copy(ints[k].at[rows, :], to, sem.at[c, b]))
            else:
                part = pl.ds(pl.multiple_of((c & 1) * 256, 256), 256)

                @pl.when(c < 2)
                def _():
                    act(pltpu.make_async_copy(ints[k].at[part, :], to, sem.at[c, b]))

                @pl.when(c >= 2)
                def _():
                    act(pltpu.make_async_copy(ints[k + 1].at[part, :], to, sem.at[c, b]))
            at += width
            k += size
        if not first:
            act(pltpu.make_async_copy(total_hbm.at[:, rows], total.at[:, rows], sem.at[c, len(sizes)]))

    whole, at = [], 0
    for k, piece in enumerate(amps_hbm):
        width = piece.shape[1]
        whole.append(pltpu.make_async_copy(piece, amps.at[:, pl.ds(at, width)], sem.at[4, k]))
        whole[-1].start()
        at += width
    for c in range(4):
        fetch(jnp.int32(c), lambda copy: copy.start())
    for copy in whole:
        copy.wait()

    def strip(c, carry):
        fetch(c, lambda copy: copy.wait())
        cols = pl.ds(pl.multiple_of(c * 256, 256), 256)

        value = dot(amps[...], rows_v[cols, :])
        if not first:
            value = value + total[:, cols]
        if not last:
            out[:, cols] = value
            return carry
        for i in range(6):
            for j in range(2):
                rows = slice(i * BLK, (i + 1) * BLK)
                tile = value[rows, j * BLK:(j + 1) * BLK] * 0.5
                on = ij_ref[i] == ab_ref[2 * c + j]
                where = pl.ds(pl.multiple_of(c * 256 + j * BLK, BLK), BLK)
                out[rows, where] = jnp.where(on, tile, jnp.zeros_like(tile)).astype(BF16)
        return carry

    lax.fori_loop(0, 4, strip, 0)


def product(sym_ij, sym_ab, amps, blocks, total=None, last=False):
    depth = sum(piece.shape[1] for piece in amps)
    first = total is None
    sizes = [len(block) for block in blocks]
    n = sum(sizes)

    def kernel(*refs):
        product_kernel(len(amps), sizes, first, last, *refs)

    scratch = [
        pltpu.VMEM((768, depth), BF16), pltpu.VMEM((1024, depth), BF16), pltpu.SemaphoreType.DMA((5, len(sizes) + 1))
    ]
    return pl.pallas_call(
        kernel,
        out_shape=jax.ShapeDtypeStruct((768, 1024), BF16 if last else F32),
        in_specs=[SMEM] * 2 + [HBM] * (len(amps) + n + (not first)),
        out_specs=VMEM,
        scratch_shapes=scratch + ([] if first else [pltpu.VMEM((768, 1024), F32)]),
        compiler_params=params(60),
        cost_estimate=cost(2 * 768 * 1024 * depth, 8 * 2**20 + 3584 * depth),
    )(sym_ij, sym_ab, *amps, *[array for block in blocks for array in block], *([] if first else [total]))


def body(amp_plus, amp_minus, ints_plus, ints_minus, sym_ij, sym_ab, sym_cd, amp_mask):
    mem = lax.axis_index("mem")
    here = jnp.stack([mem // NZ, mem % NZ]).astype(jnp.int32)

    def go(value, *waits, **way):
        return move(after(value, *waits) if waits else value, **way)

    raw_plus = lax.all_gather(amp_plus, "grp", axis=1, tiled=True)
    raw_minus = lax.all_gather(amp_minus, "grp", axis=1, tiled=True)

    z0, y0 = ints_plus, ints_minus
    zu, zd, yu, yd = [go(z0, dz=1)], [go(z0, dz=-1)], [go(y0, dy=1)], [go(y0, dy=-1)]
    ones = (zu[0], zd[0], yu[0])
    zu.append(go(zu[0], *ones, dz=1))
    zd.append(go(zd[0], *ones, dz=-1))
    y2 = (go(yu[0], *ones, yd[0], dy=1),)
    twos = (zu[1], zd[1])
    zu.append(go(zu[1], *twos, dz=1))
    zd.append(go(zd[1], *twos, dz=-1))
    c0 = join([(z0,), (zu[0],), (zd[0],), (zu[1],), (zd[1],)])
    c1 = (go(c0, *y2, dy=1), go(c0, *y2, dy=-1))
    w0 = join([(y0,), (yu[0],), (yd[0],), y2])
    threes = (zu[2], zd[2])
    wu, wd = [go(w0, *threes, dz=1)], [go(w0, *threes, dz=-1)]

    def plus(offs, *ys):
        return [(y, z) for y in ys for z in offs]

    def minus(*zs):
        return [(y, z) for z in zs for y in (0, -1, 1, 2)]

    def add(amps, blocks, *rest):
        return product(sym_ij, sym_ab, amps, blocks, *rest)

    labels = (here, sym_ij, sym_cd, amp_mask)
    near, far = (0, -1, 1, -2, 2), (-3, 3, 4)
    tp = mask(*labels, raw_plus, plus(near, 0, -1, 1) + plus(far, 0), plus(near, 2) + plus(far, -1, 1, 2))
    z4 = (go(zu[2], tp[0], dz=1),)
    d0 = join([(zu[2],), (zd[2],), z4])
    c2 = (go(c1[0][:HALF], *c1, tp[0], dy=1), go(c1[1][HALF:], *c1, tp[0], dy=-1))
    wu.append(go(wu[0], wd[0], *z4, *c1, dz=1))
    wd.append(go(wd[0], wu[0], *z4, *c1, dz=-1))
    total = add(tp[:1], [(c0,), c1[:1], c1[1:], (d0,)])
    d1 = (go(d0, *c2, total, dy=1), go(d0, *c2, total, dy=-1))
    wu.append(go(wu[1], wd[1], dz=1))
    wd.append(go(wd[1], wu[1], dz=-1))
    tm = mask(*labels, raw_minus, minus(0, -1, 1, -2, 2), minus(-3, 3), minus(4))
    d2 = (go(d1[0][:HALF], *d1, tm[0], dy=1), go(d1[1][HALF:], *d1, tm[0], dy=-1))
    total = add(tm[:1], [(w0,), (wu[0],), (wd[0],), (wu[1],), (wd[1],)], total)
    w4 = (go(wu[2][:HALF], wd[2], *d2, total, dz=1), go(wd[2][HALF:], wu[2], *d2, total, dz=-1))
    total = add([tp[1], tm[1]], [c2, d1[:1], d1[1:], d2, (wu[2],), (wd[2],)], total)
    return add(tm[2:], [w4], total, True)


def solution(mesh):
    placed = (
        P("mem", "grp"),
        P("mem", "grp"),
        P("grp", "mem"),
        P("grp", "mem"),
        P("mem"),
        P("grp"),
        P(),
        P("mem", None),
    )
    return jax.shard_map(
        body, mesh=mesh, in_specs=placed, out_specs=P("mem", "grp"), check_vma=False
    )
```

```python
import jax
import jax.numpy as jnp
from jax import lax
from jax.experimental import pallas as pl
from jax.experimental.pallas import tpu as pltpu
from jax.sharding import PartitionSpec as P

BLK = 128
NY, NZ = 4, 8
HALF = 512
BF16 = jnp.bfloat16
F32 = jnp.float32


def perm_of(dy, dz):
    return [
        (8 * y + z, 8 * ((y + dy) % NY) + (z + dz) % NZ) for y in range(NY) for z in range(NZ)
    ]


def move(values, dy=0, dz=0):
    return lax.ppermute(values, "mem", perm_of(dy, dz))


def after(value, *others):
    return lax.optimization_barrier((value,) + others)[0]


SMEM = pl.BlockSpec(memory_space=pltpu.SMEM)
VMEM = pl.BlockSpec(memory_space=pltpu.VMEM)
HBM = pl.BlockSpec(memory_space=pltpu.HBM)


def params(mib):
    return pltpu.CompilerParams(vmem_limit_bytes=mib * 2**20)


def cost(flops, moved):
    return pl.CostEstimate(flops=flops, bytes_accessed=moved, transcendentals=0)


def join_kernel(blocks, *refs):
    out, at, k = refs[-1], 0, 0
    for block in blocks:
        width = block[0].shape[1]
        if len(block) == 1:
            out[:, at:at + width] = refs[k][...]
        else:
            out[:HALF, at:at + width] = refs[k][...]
            out[HALF:, at:at + width] = refs[k + 1][...]
        at += width
        k += len(block)


def join(blocks):
    arrays = [array for block in blocks for array in block]
    full = sum(block[0].shape[1] for block in blocks)

    def kernel(*refs):
        join_kernel(blocks, *refs)

    return pl.pallas_call(
        kernel,
        out_shape=jax.ShapeDtypeStruct((2 * HALF, full), BF16),
        in_specs=[VMEM] * len(arrays),
        out_specs=VMEM,
        compiler_params=params(8),
        cost_estimate=cost(0, 8 * HALF * full),
    )(*arrays)


def dot(left, right):
    return lax.dot_general(left, right, (((1,), (1,)), ((), ())), preferred_element_type=F32)


def mask_kernel(parts, here_ref, ij_ref, cd_ref, mask_ref, raw_hbm, *refs):
    outs, raw, laid, sem = refs[:len(parts)], refs[-2 - len(parts)], refs[-1 - len(parts):-1], refs[-1]
    fetch = pltpu.make_async_copy(raw_hbm, raw, sem.at[len(parts)])
    fetch.start()
    y, z = here_ref[0], here_ref[1]
    fetch.wait()
    copies = []
    for p, (target, tiles) in enumerate(zip(laid, parts)):
        for k, (panel, off_y, off_z) in enumerate(tiles):
            tile = 8 * ((y + off_y) & (NY - 1)) + ((z + off_z) & (NZ - 1))
            cols = pl.ds(pl.multiple_of(tile * BLK, BLK), BLK)
            label = cd_ref[tile]
            for row in range(6):
                on = (ij_ref[row] == label) & (mask_ref[row, tile] == 1)
                kept = raw[panel * 768 + row * BLK:panel * 768 + (row + 1) * BLK, cols]
                target[row * BLK:(row + 1) * BLK, k * BLK:(k + 1) * BLK] = jnp.where(on, kept, jnp.zeros_like(kept))
        copies.append(pltpu.make_async_copy(target, outs[p], sem.at[p]))
        copies[-1].start()
    for copy in copies:
        copy.wait()


def mask(here, sym_ij, sym_cd, amp_mask, raw, *parts):
    shapes = [(768, len(tiles) * BLK) for tiles in parts]

    def kernel(*refs):
        mask_kernel(parts, *refs)

    return pl.pallas_call(
        kernel,
        out_shape=[jax.ShapeDtypeStruct(shape, BF16) for shape in shapes],
        in_specs=[SMEM] * 4 + [HBM],
        out_specs=[HBM] * len(shapes),
        scratch_shapes=[pltpu.VMEM((1536, 4096), BF16)]
        + [pltpu.VMEM(shape, BF16) for shape in shapes]
        + [pltpu.SemaphoreType.DMA((len(shapes) + 1,))],
        compiler_params=params(60),
        cost_estimate=cost(0, 25 * 2**20),
    )(here, sym_ij, sym_cd, amp_mask, raw)


def product_kernel(pieces, sizes, first, last, ij_ref, ab_ref, *refs):
    n = sum(sizes)
    amps_hbm, ints, refs = refs[:pieces], refs[pieces:pieces + n], refs[pieces + n:]
    if first:
        out, amps, rows_v, sem = refs
    else:
        total_hbm, out, amps, rows_v, sem, total = refs

    def fetch(c, act):
        rows = pl.ds(pl.multiple_of(c * 256, 256), 256)
        at, k = 0, 0
        for b, size in enumerate(sizes):
            width = ints[k].shape[1]
            to = rows_v.at[rows, pl.ds(at, width)]
            if size == 1:
                act(pltpu.make_async_copy(ints[k].at[rows, :], to, sem.at[c, b]))
            else:
                part = pl.ds(pl.multiple_of((c & 1) * 256, 256), 256)

                @pl.when(c < 2)
                def _():
                    act(pltpu.make_async_copy(ints[k].at[part, :], to, sem.at[c, b]))

                @pl.when(c >= 2)
                def _():
                    act(pltpu.make_async_copy(ints[k + 1].at[part, :], to, sem.at[c, b]))
            at += width
            k += size
        if not first:
            act(pltpu.make_async_copy(total_hbm.at[:, rows], total.at[:, rows], sem.at[c, len(sizes)]))

    whole, at = [], 0
    for k, piece in enumerate(amps_hbm):
        width = piece.shape[1]
        whole.append(pltpu.make_async_copy(piece, amps.at[:, pl.ds(at, width)], sem.at[4, k]))
        whole[-1].start()
        at += width
    for c in range(4):
        fetch(jnp.int32(c), lambda copy: copy.start())
    for copy in whole:
        copy.wait()

    def strip(c, carry):
        fetch(c, lambda copy: copy.wait())
        cols = pl.ds(pl.multiple_of(c * 256, 256), 256)

        value = dot(amps[...], rows_v[cols, :])
        if not first:
            value = value + total[:, cols]
        if not last:
            out[:, cols] = value
            return carry
        for i in range(6):
            for j in range(2):
                rows = slice(i * BLK, (i + 1) * BLK)
                tile = value[rows, j * BLK:(j + 1) * BLK] * 0.5
                on = ij_ref[i] == ab_ref[2 * c + j]
                where = pl.ds(pl.multiple_of(c * 256 + j * BLK, BLK), BLK)
                out[rows, where] = jnp.where(on, tile, jnp.zeros_like(tile)).astype(BF16)
        return carry

    lax.fori_loop(0, 4, strip, 0)


def product(sym_ij, sym_ab, amps, blocks, total=None, last=False):
    depth = sum(piece.shape[1] for piece in amps)
    first = total is None
    sizes = [len(block) for block in blocks]
    n = sum(sizes)

    def kernel(*refs):
        product_kernel(len(amps), sizes, first, last, *refs)

    scratch = [
        pltpu.VMEM((768, depth), BF16), pltpu.VMEM((1024, depth), BF16), pltpu.SemaphoreType.DMA((5, len(sizes) + 1))
    ]
    return pl.pallas_call(
        kernel,
        out_shape=jax.ShapeDtypeStruct((768, 1024), BF16 if last else F32),
        in_specs=[SMEM] * 2 + [HBM] * (len(amps) + n + (not first)),
        out_specs=VMEM,
        scratch_shapes=scratch + ([] if first else [pltpu.VMEM((768, 1024), F32)]),
        compiler_params=params(60),
        cost_estimate=cost(2 * 768 * 1024 * depth, 8 * 2**20 + 3584 * depth),
    )(sym_ij, sym_ab, *amps, *[array for block in blocks for array in block], *([] if first else [total]))


def body(amp_plus, amp_minus, ints_plus, ints_minus, sym_ij, sym_ab, sym_cd, amp_mask):
    mem = lax.axis_index("mem")
    here = jnp.stack([mem // NZ, mem % NZ]).astype(jnp.int32)

    def go(value, *waits, **way):
        return move(after(value, *waits) if waits else value, **way)

    raw = lax.all_gather(jnp.concatenate([amp_plus, amp_minus], axis=0), "grp", axis=1, tiled=True)

    z0, y0 = ints_plus, ints_minus
    zu, zd, yu, yd = [go(z0, dz=1)], [go(z0, dz=-1)], [go(y0, dy=1)], [go(y0, dy=-1)]
    ones = (zu[0], zd[0], yu[0])
    zu.append(go(zu[0], *ones, dz=1))
    zd.append(go(zd[0], *ones, dz=-1))
    y2 = (go(yu[0], *ones, yd[0], dy=1),)
    twos = (zu[1], zd[1])
    zu.append(go(zu[1], *twos, dz=1))
    zd.append(go(zd[1], *twos, dz=-1))
    c0 = join([(z0,), (zu[0],), (zd[0],), (zu[1],), (zd[1],)])
    c1 = (go(c0, *y2, dy=1), go(c0, *y2, dy=-1))
    w0 = join([(y0,), (yu[0],), (yd[0],), y2])
    threes = (zu[2], zd[2])
    wu, wd = [go(w0, *threes, dz=1)], [go(w0, *threes, dz=-1)]

    def plus(offs, *ys):
        return [(0, y, z) for y in ys for z in offs]

    def minus(*zs):
        return [(1, y, z) for z in zs for y in (0, -1, 1, 2)]

    def add(amps, blocks, *rest):
        return product(sym_ij, sym_ab, amps, blocks, *rest)

    near, far = (0, -1, 1, -2, 2), (-3, 3, 4)
    z4 = (go(zu[2], dz=1),)
    d0 = join([(zu[2],), (zd[2],), z4])
    c2 = (go(c1[0][:HALF], *c1, dy=1), go(c1[1][HALF:], *c1, dy=-1))
    wu.append(go(wu[0], wd[0], *z4, *c1, dz=1))
    wd.append(go(wd[0], wu[0], *z4, *c1, dz=-1))
    d1 = (go(d0, *c2, dy=1), go(d0, *c2, dy=-1))
    amps = mask(
        here, sym_ij, sym_cd, amp_mask, raw,
        plus(near, 0, -1, 1) + plus(far, 0) + minus(0, -1, 1),
        plus(near, 2) + plus(far, -1, 1) + minus(-2, 2),
        plus(far, 2) + minus(-3, 3),
        minus(4),
    )
    wu.append(go(wu[1], wd[1], amps[0], dz=1))
    wd.append(go(wd[1], wu[1], amps[0], dz=-1))
    total = add(amps[:1], [(c0,), c1[:1], c1[1:], (d0,), (w0,), (wu[0],), (wd[0],)])
    d2 = (go(d1[0][:HALF], *d1, total, dy=1), go(d1[1][HALF:], *d1, total, dy=-1))
    total = add(amps[1:2], [c2, d1[:1], d1[1:], (wu[1],), (wd[1],)], total)
    w4 = (go(wu[2][:HALF], wd[2], *d2, total, dz=1), go(wd[2][HALF:], wu[2], *d2, total, dz=-1))
    total = add(amps[2:3], [d2, (wu[2],), (wd[2],)], total)
    return add(amps[3:], [w4], total, True)


def solution(mesh):
    placed = (
        P("mem", "grp"),
        P("mem", "grp"),
        P("grp", "mem"),
        P("grp", "mem"),
        P("mem"),
        P("grp"),
        P(),
        P("mem", None),
    )
    return jax.shard_map(
        body, mesh=mesh, in_specs=placed, out_specs=P("mem", "grp"), check_vma=False
    )
```

```python
import jax
import jax.numpy as jnp
from jax import lax
from jax.experimental import pallas as pl
from jax.experimental.pallas import tpu as pltpu
from jax.sharding import PartitionSpec as P

BLK = 128
NY, NZ = 4, 8
HALF = 512
BF16 = jnp.bfloat16
F32 = jnp.float32


def perm_of(dy, dz):
    return [
        (8 * y + z, 8 * ((y + dy) % NY) + (z + dz) % NZ) for y in range(NY) for z in range(NZ)
    ]


def move(values, dy=0, dz=0):
    return lax.ppermute(values, "mem", perm_of(dy, dz))


def after(value, *others):
    return lax.optimization_barrier((value,) + others)[0]


SMEM = pl.BlockSpec(memory_space=pltpu.SMEM)
VMEM = pl.BlockSpec(memory_space=pltpu.VMEM)
HBM = pl.BlockSpec(memory_space=pltpu.HBM)


def params(mib):
    return pltpu.CompilerParams(vmem_limit_bytes=mib * 2**20)


def cost(flops, moved):
    return pl.CostEstimate(flops=flops, bytes_accessed=moved, transcendentals=0)


def join_kernel(blocks, *refs):
    out, at, k = refs[-1], 0, 0
    for block in blocks:
        width = block[0].shape[1]
        if len(block) == 1:
            out[:, at:at + width] = refs[k][...]
        else:
            out[:HALF, at:at + width] = refs[k][...]
            out[HALF:, at:at + width] = refs[k + 1][...]
        at += width
        k += len(block)


def join(blocks):
    arrays = [array for block in blocks for array in block]
    full = sum(block[0].shape[1] for block in blocks)

    def kernel(*refs):
        join_kernel(blocks, *refs)

    return pl.pallas_call(
        kernel,
        out_shape=jax.ShapeDtypeStruct((2 * HALF, full), BF16),
        in_specs=[VMEM] * len(arrays),
        out_specs=VMEM,
        compiler_params=params(8),
        cost_estimate=cost(0, 8 * HALF * full),
    )(*arrays)


def dot(left, right):
    return lax.dot_general(left, right, (((1,), (1,)), ((), ())), preferred_element_type=F32)


def mask_kernel(parts, here_ref, ij_ref, cd_ref, mask_ref, raw_hbm, *refs):
    outs, raw, laid, sem = refs[:len(parts)], refs[-2 - len(parts)], refs[-1 - len(parts):-1], refs[-1]
    fetch = pltpu.make_async_copy(raw_hbm, raw, sem.at[len(parts)])
    fetch.start()
    y, z = here_ref[0], here_ref[1]
    fetch.wait()
    copies = []
    for p, (target, tiles) in enumerate(zip(laid, parts)):
        for k, (panel, off_y, off_z) in enumerate(tiles):
            tile = 8 * ((y + off_y) & (NY - 1)) + ((z + off_z) & (NZ - 1))
            cols = pl.ds(pl.multiple_of(tile * BLK, BLK), BLK)
            label = cd_ref[tile]
            for row in range(6):
                on = (ij_ref[row] == label) & (mask_ref[row, tile] == 1)
                kept = raw[panel * 768 + row * BLK:panel * 768 + (row + 1) * BLK, cols]
                target[row * BLK:(row + 1) * BLK, k * BLK:(k + 1) * BLK] = jnp.where(on, kept, jnp.zeros_like(kept))
        copies.append(pltpu.make_async_copy(target, outs[p], sem.at[p]))
        copies[-1].start()
    for copy in copies:
        copy.wait()


def mask(here, sym_ij, sym_cd, amp_mask, raw, *parts):
    shapes = [(768, len(tiles) * BLK) for tiles in parts]

    def kernel(*refs):
        mask_kernel(parts, *refs)

    return pl.pallas_call(
        kernel,
        out_shape=[jax.ShapeDtypeStruct(shape, BF16) for shape in shapes],
        in_specs=[SMEM] * 4 + [HBM],
        out_specs=[HBM] * len(shapes),
        scratch_shapes=[pltpu.VMEM((1536, 4096), BF16)]
        + [pltpu.VMEM(shape, BF16) for shape in shapes]
        + [pltpu.SemaphoreType.DMA((len(shapes) + 1,))],
        compiler_params=params(60),
        cost_estimate=cost(0, 25 * 2**20),
    )(here, sym_ij, sym_cd, amp_mask, raw)


def product_kernel(sizes, first, last, ij_ref, ab_ref, amps_hbm, *refs):
    n = sum(sizes)
    ints, refs = refs[:n], refs[n:]
    if not first:
        total_hbm, refs = refs[0], refs[1:]
    out_hbm, amps, rows_v, total, done, sem = refs

    def fetch(c, act):
        rows = pl.ds(pl.multiple_of(c * 256, 256), 256)
        at, k = 0, 0
        for b, size in enumerate(sizes):
            width = ints[k].shape[1]
            to = rows_v.at[rows, pl.ds(at, width)]
            if size == 1:
                act(pltpu.make_async_copy(ints[k].at[rows, :], to, sem.at[c, b]))
            else:
                part = pl.ds(pl.multiple_of((c & 1) * 256, 256), 256)

                @pl.when(c < 2)
                def _():
                    act(pltpu.make_async_copy(ints[k].at[part, :], to, sem.at[c, b]))

                @pl.when(c >= 2)
                def _():
                    act(pltpu.make_async_copy(ints[k + 1].at[part, :], to, sem.at[c, b]))
            at += width
            k += size
        if not first:
            act(pltpu.make_async_copy(total_hbm.at[:, rows], total.at[:, rows], sem.at[c, len(sizes)]))

    chunks = []
    for k, at in enumerate(range(0, amps.shape[1], 1024)):
        cols = slice(at, min(at + 1024, amps.shape[1]))
        chunks.append((cols, pltpu.make_async_copy(amps_hbm.at[:, cols], amps.at[:, cols], sem.at[4, k])))
    fetch(jnp.int32(0), lambda copy: copy.start())
    for _, copy in chunks:
        copy.start()
    for c in range(1, 4):
        fetch(jnp.int32(c), lambda copy: copy.start())

    def drain(c):
        cols = pl.ds(pl.multiple_of(c * 256, 256), 256)
        return pltpu.make_async_copy(done.at[:, cols], out_hbm.at[:, cols], sem.at[5, c])

    def finish(c, value):
        cols = pl.ds(pl.multiple_of(c * 256, 256), 256)
        if not first:
            value = value + total[:, cols]
        if not last:
            done[:, cols] = value
        else:
            for i in range(6):
                for j in range(2):
                    rows = slice(i * BLK, (i + 1) * BLK)
                    tile = value[rows, j * BLK:(j + 1) * BLK] * 0.5
                    on = ij_ref[i] == ab_ref[2 * c + j]
                    where = pl.ds(pl.multiple_of(c * 256 + j * BLK, BLK), BLK)
                    done[rows, where] = jnp.where(on, tile, jnp.zeros_like(tile)).astype(BF16)
        drain(c).start()

    fetch(jnp.int32(0), lambda copy: copy.wait())
    value = None
    for cols, copy in chunks:
        copy.wait()
        part = dot(amps[:, cols], rows_v[:256, cols])
        value = part if value is None else value + part
    finish(jnp.int32(0), value)

    def strip(c, carry):
        fetch(c, lambda copy: copy.wait())
        finish(c, dot(amps[...], rows_v[pl.ds(pl.multiple_of(c * 256, 256), 256), :]))
        return carry

    lax.fori_loop(1, 4, strip, 0)
    for c in range(4):
        drain(c).wait()


def product(sym_ij, sym_ab, amps, blocks, total=None, last=False):
    depth = amps.shape[1]
    first = total is None
    sizes = [len(block) for block in blocks]
    kind = BF16 if last else F32

    def kernel(*refs):
        product_kernel(sizes, first, last, *refs)

    return pl.pallas_call(
        kernel,
        out_shape=jax.ShapeDtypeStruct((768, 1024), kind),
        in_specs=[SMEM] * 2 + [HBM] * (1 + sum(sizes) + (not first)),
        out_specs=HBM,
        scratch_shapes=[
            pltpu.VMEM((768, depth), BF16),
            pltpu.VMEM((1024, depth), BF16),
            pltpu.VMEM((8, BLK) if first else (768, 1024), F32),
            pltpu.VMEM((768, 1024), kind),
            pltpu.SemaphoreType.DMA((6, len(sizes) + 4)),
        ],
        compiler_params=params(60),
        cost_estimate=cost(2 * 768 * 1024 * depth, 8 * 2**20 + 3584 * depth),
    )(sym_ij, sym_ab, amps, *[array for block in blocks for array in block], *([] if first else [total]))


def body(amp_plus, amp_minus, ints_plus, ints_minus, sym_ij, sym_ab, sym_cd, amp_mask):
    mem = lax.axis_index("mem")
    here = jnp.stack([mem // NZ, mem % NZ]).astype(jnp.int32)

    def go(value, *waits, **way):
        return move(after(value, *waits) if waits else value, **way)

    raw = lax.all_gather(jnp.concatenate([amp_plus, amp_minus], axis=0), "grp", axis=1, tiled=True)

    z0, y0 = ints_plus, ints_minus
    zu, zd, yu, yd = [go(z0, dz=1)], [go(z0, dz=-1)], [go(y0, dy=1)], [go(y0, dy=-1)]
    ones = (zu[0], zd[0], yu[0])
    zu.append(go(zu[0], *ones, dz=1))
    zd.append(go(zd[0], *ones, dz=-1))
    y2 = (go(yu[0], *ones, yd[0], dy=1),)
    twos = (zu[1], zd[1])
    zu.append(go(zu[1], *twos, dz=1))
    zd.append(go(zd[1], *twos, dz=-1))
    c0 = join([(z0,), (zu[0],), (zd[0],), (zu[1],), (zd[1],)])
    c1 = (go(c0, *y2, dy=1), go(c0, *y2, dy=-1))
    w0 = join([(y0,), (yu[0],), (yd[0],), y2])
    threes = (zu[2], zd[2])
    wu, wd = [go(w0, *threes, dz=1)], [go(w0, *threes, dz=-1)]

    def plus(offs, *ys):
        return [(0, y, z) for y in ys for z in offs]

    def minus(*zs):
        return [(1, y, z) for z in zs for y in (0, -1, 1, 2)]

    def add(amps, blocks, *rest):
        return product(sym_ij, sym_ab, amps, blocks, *rest)

    near, far = (0, -1, 1, -2, 2), (-3, 3, 4)
    z4 = (go(zu[2], dz=1),)
    d0 = join([(zu[2],), (zd[2],), z4])
    c2 = (go(c1[0][:HALF], *c1, dy=1), go(c1[1][HALF:], *c1, dy=-1))
    wu.append(go(wu[0], wd[0], *z4, *c1, dz=1))
    wd.append(go(wd[0], wu[0], *z4, *c1, dz=-1))
    d1 = (go(d0, *c2, dy=1), go(d0, *c2, dy=-1))
    amps = mask(
        here, sym_ij, sym_cd, amp_mask, raw,
        plus(near, 0, -1, 1) + plus(far, 0) + minus(0, -1, 1),
        plus(near, 2) + plus(far, -1, 1) + minus(-2, 2),
        plus(far, 2) + minus(-3, 3),
        minus(4),
    )
    wu.append(go(wu[1], wd[1], amps[0], dz=1))
    wd.append(go(wd[1], wu[1], amps[0], dz=-1))
    total = add(amps[0], [(c0,), c1[:1], c1[1:], (d0,), (w0,), (wu[0],), (wd[0],)])
    d2 = (go(d1[0][:HALF], *d1, total, dy=1), go(d1[1][HALF:], *d1, total, dy=-1))
    total = add(amps[1], [c2, d1[:1], d1[1:], (wu[1],), (wd[1],)], total)
    w4 = (go(wu[2][:HALF], wd[2], *d2, total, dz=1), go(wd[2][HALF:], wu[2], *d2, total, dz=-1))
    total = add(amps[2], [d2, (wu[2],), (wd[2],)], total)
    return add(amps[3], [w4], total, True)


def solution(mesh):
    placed = (
        P("mem", "grp"),
        P("mem", "grp"),
        P("grp", "mem"),
        P("grp", "mem"),
        P("mem"),
        P("grp"),
        P(),
        P("mem", None),
    )
    return jax.shard_map(
        body, mesh=mesh, in_specs=placed, out_specs=P("mem", "grp"), check_vma=False
    )
```

```python
import jax
import jax.numpy as jnp
from jax import lax
from jax.experimental import pallas as pl
from jax.experimental.pallas import tpu as pltpu
from jax.sharding import PartitionSpec as P

BLK = 128
NY, NZ = 4, 8
HALF = 512
BF16 = jnp.bfloat16
F32 = jnp.float32


def perm_of(dy, dz):
    return [
        (8 * y + z, 8 * ((y + dy) % NY) + (z + dz) % NZ) for y in range(NY) for z in range(NZ)
    ]


def move(values, dy=0, dz=0):
    return lax.ppermute(values, "mem", perm_of(dy, dz))


def after(value, *others):
    return lax.optimization_barrier((value,) + others)[0]


SMEM = pl.BlockSpec(memory_space=pltpu.SMEM)
VMEM = pl.BlockSpec(memory_space=pltpu.VMEM)
HBM = pl.BlockSpec(memory_space=pltpu.HBM)


def params(mib):
    return pltpu.CompilerParams(vmem_limit_bytes=mib * 2**20)


def cost(flops, moved):
    return pl.CostEstimate(flops=flops, bytes_accessed=moved, transcendentals=0)


def join_kernel(blocks, *refs):
    out, at, k = refs[-1], 0, 0
    for block in blocks:
        width = block[0].shape[1]
        if len(block) == 1:
            out[:, at:at + width] = refs[k][...]
        else:
            out[:HALF, at:at + width] = refs[k][...]
            out[HALF:, at:at + width] = refs[k + 1][...]
        at += width
        k += len(block)


def join(blocks):
    arrays = [array for block in blocks for array in block]
    full = sum(block[0].shape[1] for block in blocks)

    def kernel(*refs):
        join_kernel(blocks, *refs)

    return pl.pallas_call(
        kernel,
        out_shape=jax.ShapeDtypeStruct((2 * HALF, full), BF16),
        in_specs=[VMEM] * len(arrays),
        out_specs=VMEM,
        compiler_params=params(8),
        cost_estimate=cost(0, 8 * HALF * full),
    )(*arrays)


def dot(left, right):
    return lax.dot_general(left, right, (((1,), (1,)), ((), ())), preferred_element_type=F32)


def mask_kernel(parts, here_ref, ij_ref, cd_ref, mask_ref, raw_hbm, *refs):
    outs, raw, laid, sem = refs[:len(parts)], refs[-2 - len(parts)], refs[-1 - len(parts):-1], refs[-1]
    fetch = pltpu.make_async_copy(raw_hbm, raw, sem.at[len(parts)])
    fetch.start()
    y, z = here_ref[0], here_ref[1]
    fetch.wait()
    copies = []
    for p, (target, tiles) in enumerate(zip(laid, parts)):
        for k, (panel, off_y, off_z) in enumerate(tiles):
            tile = 8 * ((y + off_y) & (NY - 1)) + ((z + off_z) & (NZ - 1))
            cols = pl.ds(pl.multiple_of(tile * BLK, BLK), BLK)
            label = cd_ref[tile]
            for row in range(6):
                on = (ij_ref[row] == label) & (mask_ref[row, tile] == 1)
                kept = raw[panel * 768 + row * BLK:panel * 768 + (row + 1) * BLK, cols]
                target[row * BLK:(row + 1) * BLK, k * BLK:(k + 1) * BLK] = jnp.where(on, kept, jnp.zeros_like(kept))
        copies.append(pltpu.make_async_copy(target, outs[p], sem.at[p]))
        copies[-1].start()
    for copy in copies:
        copy.wait()


def mask(here, sym_ij, sym_cd, amp_mask, raw, *parts):
    shapes = [(768, len(tiles) * BLK) for tiles in parts]

    def kernel(*refs):
        mask_kernel(parts, *refs)

    return pl.pallas_call(
        kernel,
        out_shape=[jax.ShapeDtypeStruct(shape, BF16) for shape in shapes],
        in_specs=[SMEM] * 4 + [HBM],
        out_specs=[HBM] * len(shapes),
        scratch_shapes=[pltpu.VMEM((1536, 4096), BF16)]
        + [pltpu.VMEM(shape, BF16) for shape in shapes]
        + [pltpu.SemaphoreType.DMA((len(shapes) + 1,))],
        compiler_params=params(60),
        cost_estimate=cost(0, 25 * 2**20),
    )(here, sym_ij, sym_cd, amp_mask, raw)


def product_kernel(sizes, first, last, ij_ref, ab_ref, amps_hbm, *refs):
    n = sum(sizes)
    ints, refs = refs[:n], refs[n:]
    if not first:
        total_hbm, refs = refs[0], refs[1:]
    out_hbm, amps, rows_v, total, done, sem = refs

    def fetch(c, act):
        rows = pl.ds(pl.multiple_of(c * 256, 256), 256)
        at, k = 0, 0
        for b, size in enumerate(sizes):
            width = ints[k].shape[1]
            to = rows_v.at[rows, pl.ds(at, width)]
            if size == 1:
                act(pltpu.make_async_copy(ints[k].at[rows, :], to, sem.at[c, b]))
            else:
                part = pl.ds(pl.multiple_of((c & 1) * 256, 256), 256)

                @pl.when(c < 2)
                def _():
                    act(pltpu.make_async_copy(ints[k].at[part, :], to, sem.at[c, b]))

                @pl.when(c >= 2)
                def _():
                    act(pltpu.make_async_copy(ints[k + 1].at[part, :], to, sem.at[c, b]))
            at += width
            k += size
        if not first:
            act(pltpu.make_async_copy(total_hbm.at[:, rows], total.at[:, rows], sem.at[c, len(sizes)]))

    chunks = []
    for k, at in enumerate(range(0, amps.shape[1], 1024)):
        cols = slice(at, min(at + 1024, amps.shape[1]))
        chunks.append((cols, pltpu.make_async_copy(amps_hbm.at[:, cols], amps.at[:, cols], sem.at[4, k])))
    fetch(jnp.int32(0), lambda copy: copy.start())
    for _, copy in chunks:
        copy.start()
    for c in range(1, 4):
        fetch(jnp.int32(c), lambda copy: copy.start())

    def drain(c):
        cols = pl.ds(pl.multiple_of(c * 256, 256), 256)
        return pltpu.make_async_copy(done.at[:, cols], out_hbm.at[:, cols], sem.at[5, c])

    def finish(c, value):
        cols = pl.ds(pl.multiple_of(c * 256, 256), 256)
        if not first:
            value = value + total[:, cols]
        if not last:
            done[:, cols] = value
        else:
            for i in range(6):
                for j in range(2):
                    rows = slice(i * BLK, (i + 1) * BLK)
                    tile = value[rows, j * BLK:(j + 1) * BLK] * 0.5
                    on = ij_ref[i] == ab_ref[2 * c + j]
                    where = pl.ds(pl.multiple_of(c * 256 + j * BLK, BLK), BLK)
                    done[rows, where] = jnp.where(on, tile, jnp.zeros_like(tile)).astype(BF16)
        drain(c).start()

    fetch(jnp.int32(0), lambda copy: copy.wait())
    value = None
    for cols, copy in chunks:
        copy.wait()
        part = dot(amps[:, cols], rows_v[:256, cols])
        value = part if value is None else value + part
    finish(jnp.int32(0), value)

    def strip(c, carry):
        fetch(c, lambda copy: copy.wait())
        finish(c, dot(amps[...], rows_v[pl.ds(pl.multiple_of(c * 256, 256), 256), :]))
        return carry

    lax.fori_loop(1, 4, strip, 0)
    for c in range(4):
        drain(c).wait()


def product(sym_ij, sym_ab, amps, blocks, total=None, last=False):
    depth = amps.shape[1]
    first = total is None
    sizes = [len(block) for block in blocks]
    kind = BF16 if last else F32

    def kernel(*refs):
        product_kernel(sizes, first, last, *refs)

    return pl.pallas_call(
        kernel,
        out_shape=jax.ShapeDtypeStruct((768, 1024), kind),
        in_specs=[SMEM] * 2 + [HBM] * (1 + sum(sizes) + (not first)),
        out_specs=HBM,
        scratch_shapes=[
            pltpu.VMEM((768, depth), BF16),
            pltpu.VMEM((1024, depth), BF16),
            pltpu.VMEM((8, BLK) if first else (768, 1024), F32),
            pltpu.VMEM((768, 1024), kind),
            pltpu.SemaphoreType.DMA((6, len(sizes) + 4)),
        ],
        compiler_params=params(60),
        cost_estimate=cost(2 * 768 * 1024 * depth, 8 * 2**20 + 3584 * depth),
    )(sym_ij, sym_ab, amps, *[array for block in blocks for array in block], *([] if first else [total]))


def body(amp_plus, amp_minus, ints_plus, ints_minus, sym_ij, sym_ab, sym_cd, amp_mask):
    mem = lax.axis_index("mem")
    here = jnp.stack([mem // NZ, mem % NZ]).astype(jnp.int32)

    def go(value, *waits, **way):
        return move(after(value, *waits) if waits else value, **way)

    raw = lax.all_gather(jnp.concatenate([amp_plus, amp_minus], axis=0), "grp", axis=1, tiled=True)

    z0, y0 = ints_plus, ints_minus
    zu, zd, yu, yd = [go(z0, dz=1)], [go(z0, dz=-1)], [go(y0, dy=1)], [go(y0, dy=-1)]
    ones = (zu[0], zd[0], yu[0])
    zu.append(go(zu[0], *ones, dz=1))
    zd.append(go(zd[0], *ones, dz=-1))
    y2 = (go(yu[0], *ones, yd[0], dy=1),)
    twos = (zu[1], zd[1])
    zu.append(go(zu[1], *twos, dz=1))
    zd.append(go(zd[1], *twos, dz=-1))
    c0 = join([(z0,), (zu[0],), (zd[0],), (zu[1],), (zd[1],)])
    c1 = (go(c0, *y2, dy=1), go(c0, *y2, dy=-1))
    w0 = join([(y0,), (yu[0],), (yd[0],), y2])
    threes = (zu[2], zd[2])
    wu, wd = [go(w0, *threes, dz=1)], [go(w0, *threes, dz=-1)]

    def plus(offs, *ys):
        return [(0, y, z) for y in ys for z in offs]

    def minus(*zs):
        return [(1, y, z) for z in zs for y in (0, -1, 1, 2)]

    def add(amps, blocks, *rest):
        return product(sym_ij, sym_ab, amps, blocks, *rest)

    near, far = (0, -1, 1, -2, 2), (-3, 3, 4)
    z4 = (go(zu[2], dz=1),)
    d0 = join([(zu[2],), (zd[2],), z4])
    c2 = (go(c1[0][:HALF], *c1, dy=1), go(c1[1][HALF:], *c1, dy=-1))
    wu.append(go(wu[0], wd[0], *z4, *c1, dz=1))
    wd.append(go(wd[0], wu[0], *z4, *c1, dz=-1))
    d1 = (go(d0, *c2, dy=1), go(d0, *c2, dy=-1))
    amps = mask(
        here, sym_ij, sym_cd, amp_mask, raw,
        plus(near, 0, -1, 1) + plus(far, 0) + minus(0, -1, 1),
        plus(near, 2) + plus(far, -1, 1, 2) + minus(-2, 2, -3, 3),
        minus(4),
    )
    wu.append(go(wu[1], wd[1], amps[0], dz=1))
    wd.append(go(wd[1], wu[1], amps[0], dz=-1))
    total = add(amps[0], [(c0,), c1[:1], c1[1:], (d0,), (w0,), (wu[0],), (wd[0],)])
    d2 = (go(d1[0][:HALF], *d1, dy=1), go(d1[1][HALF:], *d1, dy=-1))
    w4 = (go(wu[2][:HALF], wd[2], *d2, total, dz=1), go(wd[2][HALF:], wu[2], *d2, total, dz=-1))
    total = add(amps[1], [c2, d1[:1], d1[1:], d2, (wu[1],), (wd[1],), (wu[2],), (wd[2],)], total)
    return add(amps[2], [w4], total, True)


def solution(mesh):
    placed = (
        P("mem", "grp"),
        P("mem", "grp"),
        P("grp", "mem"),
        P("grp", "mem"),
        P("mem"),
        P("grp"),
        P(),
        P("mem", None),
    )
    return jax.shard_map(
        body, mesh=mesh, in_specs=placed, out_specs=P("mem", "grp"), check_vma=False
    )
```

```python
import jax
import jax.numpy as jnp
from jax import lax
from jax.experimental import pallas as pl
from jax.experimental.pallas import tpu as pltpu
from jax.sharding import PartitionSpec as P

BLK = 128
NY, NZ = 4, 8
HALF = 512
BF16 = jnp.bfloat16
F32 = jnp.float32


def perm_of(dy, dz):
    return [
        (8 * y + z, 8 * ((y + dy) % NY) + (z + dz) % NZ) for y in range(NY) for z in range(NZ)
    ]


def move(values, dy=0, dz=0):
    return lax.ppermute(values, "mem", perm_of(dy, dz))


def after(value, *others):
    return lax.optimization_barrier((value,) + others)[0]


SMEM = pl.BlockSpec(memory_space=pltpu.SMEM)
VMEM = pl.BlockSpec(memory_space=pltpu.VMEM)
HBM = pl.BlockSpec(memory_space=pltpu.HBM)


def params(mib):
    return pltpu.CompilerParams(vmem_limit_bytes=mib * 2**20)


def cost(flops, moved):
    return pl.CostEstimate(flops=flops, bytes_accessed=moved, transcendentals=0)


def join_kernel(blocks, *refs):
    out, at, k = refs[-1], 0, 0
    for block in blocks:
        width = block[0].shape[1]
        if len(block) == 1:
            out[:, at:at + width] = refs[k][...]
        else:
            out[:HALF, at:at + width] = refs[k][...]
            out[HALF:, at:at + width] = refs[k + 1][...]
        at += width
        k += len(block)


def join(blocks):
    arrays = [array for block in blocks for array in block]
    full = sum(block[0].shape[1] for block in blocks)

    def kernel(*refs):
        join_kernel(blocks, *refs)

    return pl.pallas_call(
        kernel,
        out_shape=jax.ShapeDtypeStruct((2 * HALF, full), BF16),
        in_specs=[VMEM] * len(arrays),
        out_specs=VMEM,
        compiler_params=params(8),
        cost_estimate=cost(0, 8 * HALF * full),
    )(*arrays)


def dot(left, right):
    return lax.dot_general(left, right, (((1,), (1,)), ((), ())), preferred_element_type=F32)


def mask_kernel(parts, here_ref, ij_ref, cd_ref, mask_ref, raw_hbm, *refs):
    outs, raw, laid, sem = refs[:len(parts)], refs[-2 - len(parts)], refs[-1 - len(parts):-1], refs[-1]
    fetch = pltpu.make_async_copy(raw_hbm, raw, sem.at[len(parts)])
    fetch.start()
    y, z = here_ref[0], here_ref[1]
    fetch.wait()
    copies = []
    for p, (target, tiles) in enumerate(zip(laid, parts)):
        for k, (panel, off_y, off_z) in enumerate(tiles):
            tile = 8 * ((y + off_y) & (NY - 1)) + ((z + off_z) & (NZ - 1))
            cols = pl.ds(pl.multiple_of(tile * BLK, BLK), BLK)
            label = cd_ref[tile]
            for row in range(6):
                on = (ij_ref[row] == label) & (mask_ref[row, tile] == 1)
                kept = raw[panel * 768 + row * BLK:panel * 768 + (row + 1) * BLK, cols]
                target[row * BLK:(row + 1) * BLK, k * BLK:(k + 1) * BLK] = jnp.where(on, kept, jnp.zeros_like(kept))
        copies.append(pltpu.make_async_copy(target, outs[p], sem.at[p]))
        copies[-1].start()
    for copy in copies:
        copy.wait()


def mask(here, sym_ij, sym_cd, amp_mask, raw, *parts):
    shapes = [(768, len(tiles) * BLK) for tiles in parts]

    def kernel(*refs):
        mask_kernel(parts, *refs)

    return pl.pallas_call(
        kernel,
        out_shape=[jax.ShapeDtypeStruct(shape, BF16) for shape in shapes],
        in_specs=[SMEM] * 4 + [HBM],
        out_specs=[HBM] * len(shapes),
        scratch_shapes=[pltpu.VMEM((1536, 4096), BF16)]
        + [pltpu.VMEM(shape, BF16) for shape in shapes]
        + [pltpu.SemaphoreType.DMA((len(shapes) + 1,))],
        compiler_params=params(60),
        cost_estimate=cost(0, 25 * 2**20),
    )(here, sym_ij, sym_cd, amp_mask, raw)


def product_kernel(sizes, first, last, ij_ref, ab_ref, amps_hbm, *refs):
    n = sum(sizes)
    ints, refs = refs[:n], refs[n:]
    if not first:
        total_hbm, refs = refs[0], refs[1:]
    out_hbm, amps, rows_v, total, done, sem = refs

    def fetch(c, act):
        rows = pl.ds(pl.multiple_of(c * 256, 256), 256)
        at, k = 0, 0
        for b, size in enumerate(sizes):
            width = ints[k].shape[1]
            to = rows_v.at[rows, pl.ds(at, width)]
            if size == 1:
                act(pltpu.make_async_copy(ints[k].at[rows, :], to, sem.at[c, b]))
            else:
                part = pl.ds(pl.multiple_of((c & 1) * 256, 256), 256)

                @pl.when(c < 2)
                def _():
                    act(pltpu.make_async_copy(ints[k].at[part, :], to, sem.at[c, b]))

                @pl.when(c >= 2)
                def _():
                    act(pltpu.make_async_copy(ints[k + 1].at[part, :], to, sem.at[c, b]))
            at += width
            k += size
        if not first:
            act(pltpu.make_async_copy(total_hbm.at[:, rows], total.at[:, rows], sem.at[c, len(sizes)]))

    chunks = []
    for k, at in enumerate(range(0, amps.shape[1], 1024)):
        cols = slice(at, min(at + 1024, amps.shape[1]))
        chunks.append((cols, pltpu.make_async_copy(amps_hbm.at[:, cols], amps.at[:, cols], sem.at[4, k])))
    fetch(jnp.int32(0), lambda copy: copy.start())
    for _, copy in chunks:
        copy.start()
    for c in range(1, 4):
        fetch(jnp.int32(c), lambda copy: copy.start())

    def drain(c):
        cols = pl.ds(pl.multiple_of(c * 256, 256), 256)
        return pltpu.make_async_copy(done.at[:, cols], out_hbm.at[:, cols], sem.at[5, c])

    def finish(c, value):
        cols = pl.ds(pl.multiple_of(c * 256, 256), 256)
        if not first:
            value = value + total[:, cols]
        if not last:
            done[:, cols] = value
        else:
            for i in range(6):
                for j in range(2):
                    rows = slice(i * BLK, (i + 1) * BLK)
                    tile = value[rows, j * BLK:(j + 1) * BLK] * 0.5
                    on = ij_ref[i] == ab_ref[2 * c + j]
                    where = pl.ds(pl.multiple_of(c * 256 + j * BLK, BLK), BLK)
                    done[rows, where] = jnp.where(on, tile, jnp.zeros_like(tile)).astype(BF16)
        drain(c).start()

    fetch(jnp.int32(0), lambda copy: copy.wait())
    value = None
    for cols, copy in chunks:
        copy.wait()
        part = dot(amps[:, cols], rows_v[:256, cols])
        value = part if value is None else value + part
    finish(jnp.int32(0), value)

    def strip(c, carry):
        fetch(c, lambda copy: copy.wait())
        finish(c, dot(amps[...], rows_v[pl.ds(pl.multiple_of(c * 256, 256), 256), :]))
        return carry

    lax.fori_loop(1, 4, strip, 0)
    for c in range(4):
        drain(c).wait()


def product(sym_ij, sym_ab, amps, blocks, total=None, last=False):
    depth = amps.shape[1]
    first = total is None
    sizes = [len(block) for block in blocks]
    kind = BF16 if last else F32

    def kernel(*refs):
        product_kernel(sizes, first, last, *refs)

    return pl.pallas_call(
        kernel,
        out_shape=jax.ShapeDtypeStruct((768, 1024), kind),
        in_specs=[SMEM] * 2 + [HBM] * (1 + sum(sizes) + (not first)),
        out_specs=HBM,
        scratch_shapes=[
            pltpu.VMEM((768, depth), BF16),
            pltpu.VMEM((1024, depth), BF16),
            pltpu.VMEM((8, BLK) if first else (768, 1024), F32),
            pltpu.VMEM((768, 1024), kind),
            pltpu.SemaphoreType.DMA((6, len(sizes) + 4)),
        ],
        compiler_params=params(60),
        cost_estimate=cost(2 * 768 * 1024 * depth, 8 * 2**20 + 3584 * depth),
    )(sym_ij, sym_ab, amps, *[array for block in blocks for array in block], *([] if first else [total]))


def body(amp_plus, amp_minus, ints_plus, ints_minus, sym_ij, sym_ab, sym_cd, amp_mask):
    mem = lax.axis_index("mem")
    here = jnp.stack([mem // NZ, mem % NZ]).astype(jnp.int32)

    def go(value, *waits, **way):
        return move(after(value, *waits) if waits else value, **way)

    raw = lax.all_gather(jnp.concatenate([amp_plus, amp_minus], axis=0), "grp", axis=1, tiled=True)

    z0, y0 = ints_plus, ints_minus
    zu, zd, yu, yd = [go(z0, dz=1)], [go(z0, dz=-1)], [go(y0, dy=1)], [go(y0, dy=-1)]
    ones = (zu[0], zd[0], yu[0])
    zu.append(go(zu[0], *ones, dz=1))
    zd.append(go(zd[0], *ones, dz=-1))
    y2 = (go(yu[0], *ones, yd[0], dy=1),)
    twos = (zu[1], zd[1])
    zu.append(go(zu[1], *twos, dz=1))
    zd.append(go(zd[1], *twos, dz=-1))
    c0 = join([(z0,), (zu[0],), (zd[0],), (zu[1],), (zd[1],)])
    c1 = (go(c0, *y2, dy=1), go(c0, *y2, dy=-1))
    w0 = join([(y0,), (yu[0],), (yd[0],), y2])
    threes = (zu[2], zd[2])
    wu, wd = [go(w0, *threes, dz=1)], [go(w0, *threes, dz=-1)]

    def plus(offs, *ys):
        return [(0, y, z) for y in ys for z in offs]

    def minus(*zs):
        return [(1, y, z) for z in zs for y in (0, -1, 1, 2)]

    def add(amps, blocks, *rest):
        return product(sym_ij, sym_ab, amps, blocks, *rest)

    near, far = (0, -1, 1, -2, 2), (-3, 3, 4)
    z4 = (go(zu[2], dz=1),)
    d0 = join([(zu[2],), (zd[2],), z4])
    c2 = (go(c1[0][:HALF], *c1, dy=1), go(c1[1][HALF:], *c1, dy=-1))
    wu.append(go(wu[0], wd[0], *z4, *c1, dz=1))
    wd.append(go(wd[0], wu[0], *z4, *c1, dz=-1))
    d1 = (go(d0, *c2, dy=1), go(d0, *c2, dy=-1))
    amps = mask(
        here, sym_ij, sym_cd, amp_mask, after(raw, *c2),
        plus(near, 0, -1, 1) + plus(far, 0) + minus(0, -1, 1),
        plus(near, 2) + plus(far, -1, 1, 2) + minus(-2, 2, -3, 3),
        minus(4),
    )
    wu.append(go(wu[1], wd[1], amps[0], dz=1))
    wd.append(go(wd[1], wu[1], amps[0], dz=-1))
    total = add(amps[0], [(c0,), c1[:1], c1[1:], (d0,), (w0,), (wu[0],), (wd[0],)])
    d2 = (go(d1[0][:HALF], *d1, dy=1), go(d1[1][HALF:], *d1, dy=-1))
    w4 = (go(wu[2][:HALF], wd[2], *d2, total, dz=1), go(wd[2][HALF:], wu[2], *d2, total, dz=-1))
    total = add(amps[1], [c2, d1[:1], d1[1:], d2, (wu[1],), (wd[1],), (wu[2],), (wd[2],)], total)
    return add(amps[2], [w4], total, True)


def solution(mesh):
    placed = (
        P("mem", "grp"),
        P("mem", "grp"),
        P("grp", "mem"),
        P("grp", "mem"),
        P("mem"),
        P("grp"),
        P(),
        P("mem", None),
    )
    return jax.shard_map(
        body, mesh=mesh, in_specs=placed, out_specs=P("mem", "grp"), check_vma=False
    )
```

```python
import jax
import jax.numpy as jnp
from jax import lax
from jax.experimental import pallas as pl
from jax.experimental.pallas import tpu as pltpu
from jax.sharding import PartitionSpec as P

BLK = 128
NY, NZ = 4, 8
HALF = 512
BF16 = jnp.bfloat16
F32 = jnp.float32


def perm_of(dy, dz):
    return [
        (8 * y + z, 8 * ((y + dy) % NY) + (z + dz) % NZ) for y in range(NY) for z in range(NZ)
    ]


def move(values, dy=0, dz=0):
    return lax.ppermute(values, "mem", perm_of(dy, dz))


def after(value, *others):
    return lax.optimization_barrier((value,) + others)[0]


SMEM = pl.BlockSpec(memory_space=pltpu.SMEM)
VMEM = pl.BlockSpec(memory_space=pltpu.VMEM)
HBM = pl.BlockSpec(memory_space=pltpu.HBM)


def params(mib):
    return pltpu.CompilerParams(vmem_limit_bytes=mib * 2**20)


def cost(flops, moved):
    return pl.CostEstimate(flops=flops, bytes_accessed=moved, transcendentals=0)


def join_kernel(blocks, *refs):
    out, at, k = refs[-1], 0, 0
    for block in blocks:
        width = block[0].shape[1]
        if len(block) == 1:
            out[:, at:at + width] = refs[k][...]
        else:
            out[:HALF, at:at + width] = refs[k][...]
            out[HALF:, at:at + width] = refs[k + 1][...]
        at += width
        k += len(block)


def join(blocks):
    arrays = [array for block in blocks for array in block]
    full = sum(block[0].shape[1] for block in blocks)

    def kernel(*refs):
        join_kernel(blocks, *refs)

    return pl.pallas_call(
        kernel,
        out_shape=jax.ShapeDtypeStruct((2 * HALF, full), BF16),
        in_specs=[VMEM] * len(arrays),
        out_specs=VMEM,
        compiler_params=params(8),
        cost_estimate=cost(0, 8 * HALF * full),
    )(*arrays)


def dot(left, right):
    return lax.dot_general(left, right, (((1,), (1,)), ((), ())), preferred_element_type=F32)


def tiles_of(terms):
    return [tile for tiles, _ in terms for tile in tiles]


def mask_kernel(parts, here_ref, ij_ref, cd_ref, mask_ref, raw_hbm, *refs):
    outs, raw, laid, sem = refs[:len(parts)], refs[-2 - len(parts)], refs[-1 - len(parts):-1], refs[-1]
    fetch = pltpu.make_async_copy(raw_hbm, raw, sem.at[len(parts)])
    fetch.start()
    y, z = here_ref[0], here_ref[1]
    fetch.wait()
    copies = []
    for p, (target, tiles) in enumerate(zip(laid, parts)):
        for k, (panel, off_y, off_z) in enumerate(tiles):
            tile = 8 * ((y + off_y) & (NY - 1)) + ((z + off_z) & (NZ - 1))
            cols = pl.ds(pl.multiple_of(tile * BLK, BLK), BLK)
            label = cd_ref[tile]
            for row in range(6):
                on = (ij_ref[row] == label) & (mask_ref[row, tile] == 1)
                kept = raw[pl.ds(panel * 768 + row * BLK, BLK), cols]
                target[row * BLK:(row + 1) * BLK, k * BLK:(k + 1) * BLK] = jnp.where(on, kept, jnp.zeros_like(kept))
        copies.append(pltpu.make_async_copy(target, outs[p], sem.at[p]))
        copies[-1].start()
    for copy in copies:
        copy.wait()


def mask(here, sym_ij, sym_cd, amp_mask, raw, groups):
    parts = [tiles_of(terms) for terms in groups]
    shapes = [(768, len(tiles) * BLK) for tiles in parts]

    def kernel(*refs):
        mask_kernel(parts, *refs)

    return pl.pallas_call(
        kernel,
        out_shape=[jax.ShapeDtypeStruct(shape, BF16) for shape in shapes],
        in_specs=[SMEM] * 4 + [HBM],
        out_specs=[HBM] * len(shapes),
        scratch_shapes=[pltpu.VMEM((1536, 4096), BF16)]
        + [pltpu.VMEM(shape, BF16) for shape in shapes]
        + [pltpu.SemaphoreType.DMA((len(shapes) + 1,))],
        compiler_params=params(60),
        cost_estimate=cost(0, 25 * 2**20),
    )(here, sym_ij, sym_cd, amp_mask, raw)


def product_kernel(sizes, first, last, ij_ref, ab_ref, amps_hbm, *refs):
    n = sum(sizes)
    ints, refs = refs[:n], refs[n:]
    if first:
        out, amps, rows_v, sem = refs
    else:
        total_hbm, out, amps, rows_v, sem, total = refs

    def fetch(c, act):
        rows = pl.ds(pl.multiple_of(c * 256, 256), 256)
        at, k = 0, 0
        for b, size in enumerate(sizes):
            width = ints[k].shape[1]
            to = rows_v.at[rows, pl.ds(at, width)]
            if size == 1:
                act(pltpu.make_async_copy(ints[k].at[rows, :], to, sem.at[c, b]))
            else:
                part = pl.ds(pl.multiple_of((c & 1) * 256, 256), 256)

                @pl.when(c < 2)
                def _():
                    act(pltpu.make_async_copy(ints[k].at[part, :], to, sem.at[c, b]))

                @pl.when(c >= 2)
                def _():
                    act(pltpu.make_async_copy(ints[k + 1].at[part, :], to, sem.at[c, b]))
            at += width
            k += size
        if not first:
            act(pltpu.make_async_copy(total_hbm.at[:, rows], total.at[:, rows], sem.at[c, len(sizes)]))

    whole = pltpu.make_async_copy(amps_hbm, amps, sem.at[4, 0])
    whole.start()
    for c in range(4):
        fetch(jnp.int32(c), lambda copy: copy.start())
    whole.wait()

    def strip(c, carry):
        fetch(c, lambda copy: copy.wait())
        cols = pl.ds(pl.multiple_of(c * 256, 256), 256)

        value = dot(amps[...], rows_v[cols, :])
        if not first:
            value = value + total[:, cols]
        if not last:
            out[:, cols] = value
            return carry
        for i in range(6):
            for j in range(2):
                rows = slice(i * BLK, (i + 1) * BLK)
                tile = value[rows, j * BLK:(j + 1) * BLK] * 0.5
                on = ij_ref[i] == ab_ref[2 * c + j]
                where = pl.ds(pl.multiple_of(c * 256 + j * BLK, BLK), BLK)
                out[rows, where] = jnp.where(on, tile, jnp.zeros_like(tile)).astype(BF16)
        return carry

    lax.fori_loop(0, 4, strip, 0)


def product(sym_ij, sym_ab, amps, terms, total=None, last=False):
    depth = amps.shape[1]
    first = total is None
    sizes = [len(block) for _, block in terms]
    n = sum(sizes)

    def kernel(*refs):
        product_kernel(sizes, first, last, *refs)

    scratch = [
        pltpu.VMEM((768, depth), BF16), pltpu.VMEM((1024, depth), BF16), pltpu.SemaphoreType.DMA((5, len(sizes) + 1))
    ]
    return pl.pallas_call(
        kernel,
        out_shape=jax.ShapeDtypeStruct((768, 1024), BF16 if last else F32),
        in_specs=[SMEM] * 2 + [HBM] * (1 + n + (not first)),
        out_specs=VMEM,
        scratch_shapes=scratch + ([] if first else [pltpu.VMEM((768, 1024), F32)]),
        compiler_params=params(60),
        cost_estimate=cost(2 * 768 * 1024 * depth, 8 * 2**20 + 3584 * depth),
    )(sym_ij, sym_ab, amps, *[array for _, block in terms for array in block], *([] if first else [total]))


def body(amp_plus, amp_minus, ints_plus, ints_minus, sym_ij, sym_ab, sym_cd, amp_mask):
    mem = lax.axis_index("mem")
    here = jnp.stack([mem // NZ, mem % NZ]).astype(jnp.int32)

    def go(value, *waits, **way):
        return move(after(value, *waits) if waits else value, **way)

    raw = lax.all_gather(jnp.concatenate([amp_plus, amp_minus], axis=0), "grp", axis=1, tiled=True)

    z0, y0 = ints_plus, ints_minus
    zu, zd, yu, yd = [go(z0, dz=1)], [go(z0, dz=-1)], [go(y0, dy=1)], [go(y0, dy=-1)]
    ones = (zu[0], zd[0], yu[0])
    zu.append(go(zu[0], *ones, dz=1))
    zd.append(go(zd[0], *ones, dz=-1))
    y2 = (go(yu[0], *ones, yd[0], dy=1),)
    twos = (zu[1], zd[1])
    zu.append(go(zu[1], *twos, dz=1))
    zd.append(go(zd[1], *twos, dz=-1))
    c0 = join([(z0,), (zu[0],), (zd[0],), (zu[1],), (zd[1],)])
    c1 = (go(c0, *y2, dy=1), go(c0, *y2, dy=-1))
    w0 = join([(y0,), (yu[0],), (yd[0],), y2])
    threes = (zu[2], zd[2])
    wu, wd = [go(w0, *threes, dz=1)], [go(w0, *threes, dz=-1)]
    z4 = (go(zu[2], dz=1),)
    d0 = join([(zu[2],), (zd[2],), z4])
    c2 = (go(c1[0][:HALF], *c1, dy=1), go(c1[1][HALF:], *c1, dy=-1))
    wu.append(go(wu[0], wd[0], *z4, dz=1))
    wd.append(go(wd[0], wu[0], *z4, dz=-1))
    d1 = (go(d0, *c2, dy=1), go(d0, *c2, dy=-1))

    def plus(offs, y, block=None):
        return [(0, y, z) for z in offs], block

    def minus(z, block=None):
        return [(1, y, z) for y in (0, -1, 1, 2)], block

    near, far = (0, -1, 1, -2, 2), (-3, 3, 4)
    groups = [
        [plus(near, y) for y in (0, -1, 1)],
        [plus(near, 2)] + [plus(far, y) for y in (0, -1, 1)] + [minus(z) for z in (0, -1, 1)],
        [plus(far, 2)] + [minus(z) for z in (-2, 2, -3, 3)],
        [minus(4)],
    ]
    amps = mask(here, sym_ij, sym_cd, amp_mask, raw, groups)
    wu.append(go(wu[1], wd[1], amps[0], dz=1))
    wd.append(go(wd[1], wu[1], amps[0], dz=-1))
    blocks = [(c0,), c1[:1], c1[1:]]
    total = product(sym_ij, sym_ab, amps[0], [(None, block) for block in blocks])
    d2 = (go(d1[0][:HALF], *d1, total, dy=1), go(d1[1][HALF:], *d1, total, dy=-1))
    blocks = [c2, (d0,), d1[:1], d1[1:], (w0,), (wu[0],), (wd[0],)]
    total = product(sym_ij, sym_ab, amps[1], [(None, block) for block in blocks], total)
    w4 = (go(wu[2][:HALF], wd[2], *d2, total, dz=1), go(wd[2][HALF:], wu[2], *d2, total, dz=-1))
    blocks = [d2, (wu[1],), (wd[1],), (wu[2],), (wd[2],)]
    total = product(sym_ij, sym_ab, amps[2], [(None, block) for block in blocks], total)
    return product(sym_ij, sym_ab, amps[3], [(None, w4)], total, True)


def solution(mesh):
    placed = (
        P("mem", "grp"),
        P("mem", "grp"),
        P("grp", "mem"),
        P("grp", "mem"),
        P("mem"),
        P("grp"),
        P(),
        P("mem", None),
    )
    return jax.shard_map(
        body, mesh=mesh, in_specs=placed, out_specs=P("mem", "grp"), check_vma=False
    )
```
